32 devices in a mesh: orb: 4 (over y, core), aux: 8 (over z, x).
Axes of the slice: x: 2, y: 2, z: 4, core: 2. Of those that a mesh axis runs over, the one named last changes fastest.
Arguments:
- factors: bfloat16 [192, 128, 2048], P('orb', None, 'aux'), may hold values from -6 to 6
- amplitudes: bfloat16 [192, 12, 128, 128], P('orb'), may hold values from -0.15625 to 0.15625
- partners: int32 [192, 12], P('orb'), may hold values from 0 to 191, as said below
- metric_tiles: bfloat16 [128, 128, 128], P('aux'), may hold values from -0.1875 to 0.1875
- tile_pos: int32 [128, 2], P('aux'), may hold values from 0 to 15, as said below
Outputs:
- density: bfloat16 [192, 128, 2048], P('orb', 'aux')
The draws below stay inside these ranges and needn't reach their ends.
Inputs may be any that keep to these rules, and one draw needn't show every extreme that they name: partners[i, 0] = i for every orbital i; the other partners of an orbital are any orbitals, repeats allowed. `tile_pos`: the listed positions (row block, column block) are all distinct, and each of the 16 diagonal positions is listed.
All inputs are finite; a program needn't handle non-finite values.
Results may differ from the reference program's by a relative error of at most 0.0049.
Values may be sent and summed in bfloat16 or wider, within the bound.
No kernel may reach another device: no remote copies, remote signals or barrier semaphores. Data moves between devices by JAX's collectives and lax.ppermute only.
A program may use at most 192 MiB of HBM per device.

```python
import jax
import jax.numpy as jnp
from jax import lax

NVD = 128
AUX = 2048
TILE = 128
PAIRS = 12
NTILE = 128
OCC = 192
NBLK = 16


def draw_partners(key, part):
    orbitals = jnp.arange(OCC, dtype=jnp.int32)
    others = jax.random.randint(jax.random.fold_in(key, 11), (OCC, PAIRS - 1), 0, OCC, dtype=jnp.int32)
    return jnp.concatenate([orbitals[:, None], others], axis=1).astype(jnp.int32)


def draw_tile_pos(key, part):
    cells = jnp.arange(NBLK * NBLK, dtype=jnp.int32)
    row_ids = cells // NBLK
    col_ids = cells % NBLK
    scores = jax.random.permutation(jax.random.fold_in(key, 21), NBLK * NBLK).astype(jnp.int32)
    scores = jnp.where(row_ids != col_ids, scores + 1, jnp.zeros_like(scores))
    order = jnp.argsort(scores, stable=True)[:NTILE]
    chosen = jnp.take(cells, order)
    shuffle = jax.random.permutation(jax.random.fold_in(key, 22), NTILE)
    chosen = jnp.take(chosen, shuffle)
    return jnp.stack([chosen // NBLK, chosen % NBLK], axis=1).astype(jnp.int32)


def block_levels(rng, shape, shards, low, high):
    gain, own = 1.0, jax.random.fold_in(rng, 6)
    for axis_at, shards_of in shards:
        draws = jnp.exp(jax.random.uniform(jax.random.fold_in(own, axis_at), (shards_of,), jnp.float32, low / len(shards), high / len(shards)))
        gain = gain * jnp.repeat(draws, shape[axis_at] // shards_of).reshape([-1 if axis == axis_at else 1 for axis in range(len(shape))])
    return gain


def normal_values(stream_key, extent, width, reach, split=(), kind=jnp.bfloat16):
    array = width * jax.random.normal(stream_key, extent, jnp.float32)
    if split:
        array = array * block_levels(stream_key, extent, split, -0.22, 0.18)
    return jnp.clip(array, -reach, reach).astype(kind)


def setup_inputs(seed: int = 0) -> dict:
    seeds = jax.random.split(jax.random.key(seed), 6)
    factors = normal_values(seeds[0], (OCC, NVD, AUX), 1.0, 6.0, ((0, 4), (2, 8)))
    amplitudes = normal_values(seeds[1], (OCC, PAIRS, NVD, NVD), (PAIRS * NVD) ** -0.5, 0.15625, ((0, 4),))
    partners = draw_partners(jax.random.fold_in(seeds[5], 71), 0)
    metric_tiles = normal_values(seeds[3], (NTILE, TILE, TILE), (TILE * NTILE // NBLK) ** -0.5, 0.1875, ((0, 8),))
    tile_pos = draw_tile_pos(jax.random.fold_in(seeds[5], 71), 0)
    return dict(factors=factors, amplitudes=amplitudes, partners=partners, metric_tiles=metric_tiles, tile_pos=tile_pos)


def reference(factors, amplitudes, partners, metric_tiles, tile_pos):
    def one_orbital(inputs):
        amp_tiles, partner_ids = inputs
        picked = jnp.take(factors, partner_ids, axis=0).astype(jnp.float32)
        summed = jnp.einsum("kab,kbp->ap", amp_tiles.astype(jnp.float32), picked, precision=lax.Precision.HIGHEST)
        return summed.astype(jnp.bfloat16)

    gammas = lax.map(one_orbital, (amplitudes, partners))
    full_metric = jnp.zeros((NBLK, NBLK, TILE, TILE), jnp.float32)
    full_metric = full_metric.at[tile_pos[:, 0], tile_pos[:, 1]].add(metric_tiles.astype(jnp.float32))
    full_metric = full_metric.transpose(0, 2, 1, 3).reshape(AUX, AUX)
    row_block = gammas.reshape(OCC * NVD, AUX).astype(jnp.float32)
    product = jnp.dot(row_block, full_metric, precision=lax.Precision.HIGHEST)
    return product.reshape(OCC, NVD, AUX).astype(jnp.bfloat16)
```

```python
import functools

import jax
import jax.numpy as jnp
from jax import lax
from jax.experimental import pallas as pl
from jax.experimental.pallas import tpu as pltpu
from jax.sharding import PartitionSpec as P

VMEM_LIMIT = 40 * 1024 * 1024


def largest_divisor(total, most):
    return max(size for size in range(1, most + 1) if total % size == 0)


def pack_kernel(width, source, *chunks):
    half = source.shape[1] // 2
    for at, chunk in enumerate(chunks):
        columns = slice(at * width, (at + 1) * width)
        chunk[...] = jnp.concatenate([source[:, :half, columns], source[:, half:, columns]], axis=-1)


def pack_chunks(factors, width):
    orbitals, domain, part = factors.shape
    count = part // width
    step = largest_divisor(orbitals, 8)
    packed = (step, domain // 2, 2 * width)
    return pl.pallas_call(
        functools.partial(pack_kernel, width),
        grid=(orbitals // step,),
        in_specs=[pl.BlockSpec((step, domain, part), lambda i: (i, 0, 0))],
        out_specs=[pl.BlockSpec(packed, lambda i: (i, 0, 0))] * count,
        out_shape=[jax.ShapeDtypeStruct((orbitals,) + packed[1:], factors.dtype)] * count,
        cost_estimate=pl.CostEstimate(flops=0, bytes_accessed=4 * factors.size, transcendentals=0),
        compiler_params=pltpu.CompilerParams(vmem_limit_bytes=VMEM_LIMIT),
        name="pack_chunks",
    )(factors)


def product_kernel(pairs, split_rows, slots, amplitudes, *refs):
    pieces = refs[: -4]
    out, staged, table, arrived = refs[-4:]
    group, half_domain, lanes = pieces[0].shape
    width = lanes // 2
    here = pl.program_id(0)

    @pl.when(here == 0)
    def _():
        copies = [
            pltpu.make_async_copy(piece, staged.at[pl.ds(at * group, group)], arrived.at[at])
            for at, piece in enumerate(pieces)
        ]
        for copy in copies:
            copy.start()
        for at, copy in enumerate(copies):
            copy.wait()

            @pl.loop(at * group, (at + 1) * group, unroll=4)
            def _(row):
                block = staged[row]
                table[row, :half_domain, :] = block[:, :width]
                table[row, half_domain:, :] = block[:, width:]

    step = amplitudes.shape[1]
    half_count = pl.num_programs(0) * step

    @pl.loop(0, step)
    def _(q):
        sums = []
        for side in range(2):
            base = (side * half_count + here * step + q) * pairs
            left = jnp.concatenate([amplitudes[side, q, k] for k in range(pairs)], axis=1)
            right = jnp.concatenate([table[slots[base + k]] for k in range(pairs)], axis=0)
            sums.append(jnp.dot(left, right, preferred_element_type=jnp.float32))
        both = jnp.concatenate(sums, axis=1).astype(out.dtype)
        if split_rows:
            owners, rows = out.shape[0], both.shape[0] // out.shape[0]
            out[:, pl.ds(pl.multiple_of(q * rows, rows), rows), :] = both.reshape(owners, rows, lanes)
        else:
            out[q] = both


def chunk_products(slots, amplitudes, pieces, owners):
    orbitals, pairs, domain, _ = amplitudes.shape
    group, half_domain, lanes = pieces[0].shape
    total = group * len(pieces)
    half = orbitals // 2
    rows = domain // owners
    split_rows = rows % 16 == 0
    step = largest_divisor(half, 4)
    if split_rows:
        out_shape, out_block, out_at = (owners, half * rows, lanes), (owners, step * rows, lanes), lambda i, s: (0, i, 0)
    else:
        out_shape, out_block, out_at = (half, domain, lanes), (step, domain, lanes), lambda i, s: (i, 0, 0)
    result = pl.pallas_call(
        functools.partial(product_kernel, pairs, split_rows),
        grid_spec=pltpu.PrefetchScalarGridSpec(
            num_scalar_prefetch=1,
            grid=(half // step,),
            in_specs=[pl.BlockSpec((2, step, pairs, domain, domain), lambda i, s: (0, i, 0, 0, 0))]
            + [pl.BlockSpec(memory_space=pl.ANY)] * len(pieces),
            out_specs=pl.BlockSpec(out_block, out_at),
            scratch_shapes=[
                pltpu.VMEM((total, half_domain, lanes), jnp.bfloat16),
                pltpu.VMEM((total, domain, lanes // 2), jnp.bfloat16),
                pltpu.SemaphoreType.DMA((len(pieces),)),
            ],
        ),
        out_shape=jax.ShapeDtypeStruct(out_shape, jnp.bfloat16),
        cost_estimate=pl.CostEstimate(
            flops=4 * amplitudes.size * (lanes // 2),
            bytes_accessed=2 * amplitudes.size + 2 * total * half_domain * lanes,
            transcendentals=0,
        ),
        compiler_params=pltpu.CompilerParams(vmem_limit_bytes=VMEM_LIMIT),
        name="chunk_products",
    )(slots, amplitudes.reshape(2, half, pairs, domain, domain), *pieces)
    if split_rows:
        return result
    result = result.reshape(half, owners, rows, lanes).transpose(1, 0, 2, 3)
    return result.reshape(owners, half * rows, lanes)


def place_kernel(chunks, owners, tiles_each, positions, first, second, out):
    span = first.shape[2]
    width = span // 2
    out[...] = jnp.zeros_like(out)
    for which, source in enumerate((first, second)):

        @pl.loop(0, source.shape[0])
        def _(device):
            @pl.loop(0, tiles_each)
            def _(at):
                number = (which * owners + device) * tiles_each + at
                column = pl.multiple_of(positions[2 * number + 1] * span, span)
                for side in range(2):
                    block = 2 * positions[2 * number] + side
                    row = ((block % chunks) * owners + block // chunks) * width
                    begin = pl.multiple_of(at * span + side * width, width)
                    out[pl.ds(pl.multiple_of(row, width), width), pl.ds(column, span)] = source[
                        device, pl.ds(begin, width), :
                    ]


def place_tiles(positions, first, second, tiles_each, chunks, size):
    owners = first.shape[0]
    return pl.pallas_call(
        functools.partial(place_kernel, chunks, owners, tiles_each),
        grid_spec=pltpu.PrefetchScalarGridSpec(
            num_scalar_prefetch=1,
            grid=(1,),
            in_specs=[pl.BlockSpec(first.shape, lambda i, s: (0, 0, 0))] * 2,
            out_specs=pl.BlockSpec((size, size), lambda i, s: (0, 0)),
        ),
        out_shape=jax.ShapeDtypeStruct((size, size), first.dtype),
        cost_estimate=pl.CostEstimate(flops=0, bytes_accessed=4 * first.size + 2 * size * size, transcendentals=0),
        compiler_params=pltpu.CompilerParams(vmem_limit_bytes=VMEM_LIMIT),
        name="place_tiles",
    )(positions, first, second)


def metric_kernel(*refs):
    chunks = refs[:-3]
    metric, out, rows = refs[-3], refs[-2], refs[-1]
    owners, height, lanes = chunks[0].shape
    width = lanes // 2

    @pl.when(pl.program_id(0) == 0)
    def _():
        for at, chunk in enumerate(chunks):
            for owner in range(0, owners, 2):
                one, two = chunk[owner], chunk[owner + 1]
                columns = pl.ds((at * owners + owner) * width, lanes)
                rows[:height, columns] = jnp.concatenate([one[:, :width], two[:, :width]], axis=1)
                rows[height:, columns] = jnp.concatenate([one[:, width:], two[:, width:]], axis=1)

    sums = jnp.dot(rows[...], metric[...], preferred_element_type=jnp.float32).astype(out.dtype)
    out[0] = sums[:height]
    out[1] = sums[height:]


def apply_metric(chunks, metric):
    owners, height, lanes = chunks[0].shape
    size = metric.shape[0]
    step = largest_divisor(size, 256)
    return pl.pallas_call(
        metric_kernel,
        grid=(size // step,),
        in_specs=[pl.BlockSpec((owners, height, lanes), lambda j: (0, 0, 0))] * len(chunks)
        + [pl.BlockSpec((size, step), lambda j: (0, j))],
        out_specs=pl.BlockSpec((2, height, step), lambda j: (0, 0, j)),
        out_shape=jax.ShapeDtypeStruct((2, height, size), jnp.bfloat16),
        scratch_shapes=[pltpu.VMEM((2 * height, size), jnp.bfloat16)],
        cost_estimate=pl.CostEstimate(
            flops=4 * height * size * size,
            bytes_accessed=2 * size * size + 8 * height * size,
            transcendentals=0,
        ),
        compiler_params=pltpu.CompilerParams(vmem_limit_bytes=VMEM_LIMIT),
        name="apply_metric",
    )(*chunks, metric)


def shards(orb_count, aux_count, factors, amplitudes, partners, metric_tiles, tile_pos):
    group, domain, part = factors.shape
    span = metric_tiles.shape[1]
    width = span // 2
    chunk_count = part // width
    far_count = orb_count // 2
    me = lax.axis_index("orb")

    def to_far(array, shift):
        moves = [(g, (g + 2 * shift) % orb_count) for g in range(orb_count)]
        return lax.ppermute(array, "orb", moves)

    def to_mate(array):
        return lax.ppermute(array, "orb", [(g, g ^ 1) for g in range(orb_count)])

    owner, place = partners // group, partners % group
    far = (me // 2 - owner // 2) % far_count
    slots = ((far * 2 + (me % 2 + owner) % 2) * group + place).reshape(-1)

    half_tiles = metric_tiles.shape[0] // 2
    mine = (me % 2) * half_tiles
    tiles = lax.dynamic_slice_in_dim(metric_tiles, mine, half_tiles, axis=0).reshape(half_tiles * span, span)
    spots = lax.dynamic_slice_in_dim(tile_pos, mine, half_tiles, axis=0).reshape(-1).astype(tiles.dtype)
    spot_rows = -(-spots.size // (16 * span)) * 16
    spots = jnp.pad(spots, (0, spot_rows * span - spots.size)).reshape(spot_rows, span)
    load = jnp.concatenate([tiles, spots], axis=0)

    packed = pack_chunks(factors, width)
    sent = []
    products = []
    last = None
    for at in range(chunk_count):
        own = packed[at]
        if last is not None:
            own, last = lax.optimization_barrier((own, last))
        far_pieces = [to_far(own, shift) for shift in range(1, far_count)]
        last = far_pieces[-1] if far_pieces else None
        pieces = []
        for piece in [own] + far_pieces:
            pieces += [piece, to_mate(piece)]
        made = chunk_products(slots, amplitudes, pieces, aux_count)
        products.append(lax.all_to_all(made, "aux", split_axis=0, concat_axis=0, tiled=True))

    parts = [load[None]]
    for shift in range(1, aux_count // 2):
        moves = [(g, (g + 2 * shift) % aux_count) for g in range(aux_count)]
        parts.append(lax.ppermute(load[None], "aux", moves))
    column = jnp.concatenate(parts, axis=0)
    beside = lax.ppermute(column, "aux", [(g, g ^ 1) for g in range(aux_count)])
    first = jnp.concatenate([column, beside], axis=0)
    second = to_mate(first)
    positions = jnp.stack([first[:, half_tiles * span :], second[:, half_tiles * span :]])
    positions = positions.reshape(2 * aux_count, -1)[:, : 2 * half_tiles].astype(jnp.int32).reshape(-1)
    metric = place_tiles(positions, first, second, half_tiles, chunk_count, part * aux_count)

    result = apply_metric(products, metric)
    return result.reshape(group, domain // aux_count, part * aux_count)


def solution(mesh):
    in_specs = (
        P("orb", None, "aux"),
        P("orb", None, None, None),
        P("orb", None),
        P("aux", None, None),
        P("aux", None),
    )
    body = functools.partial(shards, mesh.shape["orb"], mesh.shape["aux"])
    return jax.shard_map(body, mesh=mesh, in_specs=in_specs, out_specs=P("orb", "aux", None), check_vma=False)
```

```python
import functools

import jax
import jax.numpy as jnp
from jax import lax
from jax.experimental import pallas as pl
from jax.experimental.pallas import tpu as pltpu
from jax.sharding import PartitionSpec as P

VMEM_LIMIT = 40 * 1024 * 1024
VMEM_WHOLE = 58 * 1024 * 1024


def largest_divisor(total, most):
    return max(size for size in range(1, most + 1) if total % size == 0)


def pack_kernel(first, width, source, chunk):
    half = source.shape[1] // 2
    columns = slice(first, first + width)
    chunk[...] = jnp.concatenate([source[:, :half, columns], source[:, half:, columns]], axis=-1)


def pack_chunk(factors, width, at):
    orbitals, domain, part = factors.shape
    lanes = 2 * width if part % (2 * width) == 0 else part
    step = largest_divisor(orbitals, 16)
    first = at * width
    return pl.pallas_call(
        functools.partial(pack_kernel, first % lanes, width),
        grid=(orbitals // step,),
        in_specs=[pl.BlockSpec((step, domain, lanes), lambda i: (i, 0, first // lanes))],
        out_specs=pl.BlockSpec((step, domain // 2, 2 * width), lambda i: (i, 0, 0)),
        out_shape=jax.ShapeDtypeStruct((orbitals, domain // 2, 2 * width), factors.dtype),
        cost_estimate=pl.CostEstimate(flops=0, bytes_accessed=6 * orbitals * domain * width, transcendentals=0),
        compiler_params=pltpu.CompilerParams(vmem_limit_bytes=VMEM_WHOLE),
        name="pack_chunk",
    )(factors)


def product_kernel(pairs, split_rows, slots, amplitudes, *refs):
    pieces = refs[:-3]
    out, table, arrived = refs[-3:]
    group, half_domain, lanes = pieces[0].shape
    here = pl.program_id(0)

    @pl.when(here == 0)
    def _():
        copies = [
            pltpu.make_async_copy(piece, table.at[pl.ds(at * group, group), pl.ds(0, half_domain)], arrived.at[at])
            for at, piece in enumerate(pieces)
        ]
        for copy in copies:
            copy.start()
        for at, copy in enumerate(copies):
            copy.wait()

            @pl.loop(at * group, (at + 1) * group, unroll=8)
            def _(row):
                block = table[row, :half_domain, :]
                table[row, half_domain:, :] = jnp.concatenate([block[:, lanes // 2 :], block[:, : lanes // 2]], axis=1)

    step = amplitudes.shape[1]
    half_count = pl.num_programs(0) * step
    lower = lax.broadcasted_iota(jnp.int32, (amplitudes.shape[3], lanes), 1) < lanes // 2
    for q in range(step):
        sums = []
        for side in range(2):
            base = (side * half_count + here * step + q) * pairs
            left = jnp.concatenate([amplitudes[side, q, k] for k in range(pairs)], axis=1)
            right = []
            for k in range(pairs):
                slot = slots[base + k]
                if side:
                    right += [table[slot, half_domain:, :], table[slot, :half_domain, :]]
                else:
                    right += [table[slot]]
            sums.append(jnp.dot(left, jnp.concatenate(right, axis=0), preferred_element_type=jnp.float32))
        both = jnp.where(lower, sums[0], sums[1]).astype(out.dtype)
        if split_rows:
            owners, rows = out.shape[0], both.shape[0] // out.shape[0]
            out[:, q * rows : (q + 1) * rows, :] = both.reshape(owners, rows, lanes)
        else:
            out[q] = both


def chunk_products(slots, amplitudes, pieces, owners):
    orbitals, pairs, domain, _ = amplitudes.shape
    group, half_domain, lanes = pieces[0].shape
    total = group * len(pieces)
    half = orbitals // 2
    rows = domain // owners
    split_rows = rows % 16 == 0
    step = largest_divisor(half, 4)
    if split_rows:
        out_shape, out_block, out_at = (owners, half * rows, lanes), (owners, step * rows, lanes), lambda i, s: (0, i, 0)
    else:
        out_shape, out_block, out_at = (half, domain, lanes), (step, domain, lanes), lambda i, s: (i, 0, 0)
    result = pl.pallas_call(
        functools.partial(product_kernel, pairs, split_rows),
        grid_spec=pltpu.PrefetchScalarGridSpec(
            num_scalar_prefetch=1,
            grid=(half // step,),
            in_specs=[pl.BlockSpec((2, step, pairs, domain, domain), lambda i, s: (0, i, 0, 0, 0))]
            + [pl.BlockSpec(memory_space=pl.ANY)] * len(pieces),
            out_specs=pl.BlockSpec(out_block, out_at),
            scratch_shapes=[
                pltpu.VMEM((total, domain, lanes), jnp.bfloat16),
                pltpu.SemaphoreType.DMA((len(pieces),)),
            ],
        ),
        out_shape=jax.ShapeDtypeStruct(out_shape, jnp.bfloat16),
        cost_estimate=pl.CostEstimate(
            flops=8 * amplitudes.size * lanes,
            bytes_accessed=2 * amplitudes.size + 2 * total * half_domain * lanes,
            transcendentals=0,
        ),
        compiler_params=pltpu.CompilerParams(vmem_limit_bytes=VMEM_LIMIT),
        name="chunk_products",
    )(slots, amplitudes.reshape(2, half, pairs, domain, domain), *pieces)
    if split_rows:
        return result
    result = result.reshape(half, owners, rows, lanes).transpose(1, 0, 2, 3)
    return result.reshape(owners, half * rows, lanes)


def join_kernel(*refs):
    pieces = refs[:-2]
    out, arrived = refs[-2:]
    copies = [pltpu.make_async_copy(piece, out.at[at], arrived.at[at]) for at, piece in enumerate(pieces)]
    for copy in copies:
        copy.start()
    for copy in copies:
        copy.wait()


def join(pieces):
    shape = (len(pieces),) + pieces[0].shape
    return pl.pallas_call(
        join_kernel,
        in_specs=[pl.BlockSpec(memory_space=pl.ANY)] * len(pieces),
        out_specs=pl.BlockSpec(memory_space=pl.ANY),
        out_shape=jax.ShapeDtypeStruct(shape, pieces[0].dtype),
        scratch_shapes=[pltpu.SemaphoreType.DMA((len(pieces),))],
        cost_estimate=pl.CostEstimate(flops=0, bytes_accessed=4 * len(pieces) * pieces[0].size, transcendentals=0),
        name="join",
    )(*pieces)


def place_kernel(chunks, owners, tiles_each, positions, *refs):
    sources, out = refs[:-1], refs[-1]
    devices, _, span = sources[0].shape
    width = span // 2
    out[...] = jnp.zeros_like(out)
    for which, source in enumerate(sources):

        @pl.loop(0, devices)
        def _(device):
            for at in range(tiles_each):
                number = (which * devices + device) * tiles_each + at
                column = pl.multiple_of(positions[2 * number + 1] * span, span)
                for side in range(2):
                    block = 2 * positions[2 * number] + side
                    row = ((block % chunks) * owners + block // chunks) * width
                    begin = at * span + side * width
                    out[pl.ds(pl.multiple_of(row, width), width), pl.ds(column, span)] = source[
                        device, begin : begin + width, :
                    ]


def place_tiles(positions, sources, tiles_each, chunks, owners, size):
    shape = sources[0].shape
    return pl.pallas_call(
        functools.partial(place_kernel, chunks, owners, tiles_each),
        grid_spec=pltpu.PrefetchScalarGridSpec(
            num_scalar_prefetch=1,
            grid=(1,),
            in_specs=[pl.BlockSpec(shape, lambda i, s: (0, 0, 0))] * len(sources),
            out_specs=pl.BlockSpec((size, size), lambda i, s: (0, 0)),
        ),
        out_shape=jax.ShapeDtypeStruct((size, size), sources[0].dtype),
        cost_estimate=pl.CostEstimate(
            flops=0, bytes_accessed=2 * len(sources) * sources[0].size + 2 * size * size, transcendentals=0
        ),
        compiler_params=pltpu.CompilerParams(vmem_limit_bytes=VMEM_LIMIT),
        name="place_tiles",
    )(positions, *sources)


def metric_kernel(count, has_before, *refs):
    chunks, metric, before = refs[:count], refs[count], refs[count + 1]
    out, rows = refs[-2:]
    owners, height, lanes = chunks[0].shape
    width = lanes // 2

    @pl.when(pl.program_id(0) == 0)
    def _():
        for at, chunk in enumerate(chunks):
            for owner in range(0, owners, 2):
                one, two = chunk[owner], chunk[owner + 1]
                columns = pl.ds((at * owners + owner) * width, lanes)
                rows[:height, columns] = jnp.concatenate([one[:, :width], two[:, :width]], axis=1)
                rows[height:, columns] = jnp.concatenate([one[:, width:], two[:, width:]], axis=1)

    for side in range(2):
        sums = jnp.dot(rows[side * height : (side + 1) * height], metric[...], preferred_element_type=jnp.float32)
        if has_before:
            sums += before[side]
        out[side] = sums.astype(out.dtype)


def apply_metric(chunks, metric, begin, before, dtype):
    owners, height, lanes = chunks[0].shape
    size = metric.shape[0]
    depth = len(chunks) * owners * lanes // 2
    step = largest_divisor(size, 256)
    sums = [] if before is None else [before]
    block = pl.BlockSpec((2, height, step), lambda j: (0, 0, j))
    return pl.pallas_call(
        functools.partial(metric_kernel, len(chunks), before is not None),
        grid=(size // step,),
        in_specs=[pl.BlockSpec((owners, height, lanes), lambda j: (0, 0, 0))] * len(chunks)
        + [pl.BlockSpec((depth, step), lambda j: (begin // len(chunks), j))]
        + [block] * len(sums),
        out_specs=block,
        out_shape=jax.ShapeDtypeStruct((2, height, size), dtype),
        scratch_shapes=[pltpu.VMEM((2 * height, depth), jnp.bfloat16)],
        cost_estimate=pl.CostEstimate(
            flops=4 * height * depth * size,
            bytes_accessed=2 * depth * size + 12 * height * size,
            transcendentals=0,
        ),
        compiler_params=pltpu.CompilerParams(vmem_limit_bytes=VMEM_LIMIT),
        name="apply_metric",
    )(*chunks, metric, *sums)


def after(value, others):
    return lax.optimization_barrier((value, others))[0]


def shards(orb_count, aux_count, factors, amplitudes, partners, metric_tiles, tile_pos):
    group, domain, part = factors.shape
    span = metric_tiles.shape[1]
    width = span // 2
    chunk_count = part // width
    far_count = orb_count // 2
    me = lax.axis_index("orb")

    def to_far(array, shift):
        moves = [(g, (g + 2 * shift) % orb_count) for g in range(orb_count)]
        return lax.ppermute(array, "orb", moves)

    def to_mate(array):
        return lax.ppermute(array, "orb", [(g, g ^ 1) for g in range(orb_count)])

    owner, place = partners // group, partners % group
    far = (me // 2 - owner // 2) % far_count
    slots = ((far * 2 + (me % 2 + owner) % 2) * group + place).reshape(-1)

    half_tiles = metric_tiles.shape[0] // 2
    mine = (me % 2) * half_tiles
    tiles = lax.dynamic_slice_in_dim(metric_tiles, mine, half_tiles, axis=0).reshape(half_tiles * span, span)
    spots = lax.dynamic_slice_in_dim(tile_pos, mine, half_tiles, axis=0).reshape(-1).astype(tiles.dtype)
    spot_rows = -(-spots.size // (16 * span)) * 16
    spots = jnp.pad(spots, (0, spot_rows * span - spots.size)).reshape(spot_rows, span)
    load = jnp.concatenate([tiles, spots], axis=0)
    parts = [load]
    for shift in range(1, aux_count // 2):
        moves = [(g, (g + 2 * shift) % aux_count) for g in range(aux_count)]
        parts.append(lax.ppermute(load, "aux", moves))

    products = []
    last = None
    for at in range(chunk_count):
        own = pack_chunk(factors, width, at)
        if last is not None:
            own = after(own, last)
        far_pieces = [to_far(own, shift) for shift in range(1, far_count)]
        last = far_pieces[-1] if far_pieces else None
        pieces = []
        for piece in [own] + far_pieces:
            pieces += [piece, to_mate(piece)]
        made = chunk_products(slots, amplitudes, pieces, aux_count)
        if at == 0:
            made = after(made, parts)
        products.append(lax.all_to_all(made, "aux", split_axis=0, concat_axis=0, tiled=True))

    column = join(parts)
    beside = lax.ppermute(column, "aux", [(g, g ^ 1) for g in range(aux_count)])
    sources = [column, beside, to_mate(column), to_mate(beside)]
    positions = jnp.concatenate([source[:, half_tiles * span, : 2 * half_tiles] for source in sources])
    positions = positions.astype(jnp.int32).reshape(-1)
    metric = place_tiles(positions, sources, half_tiles, chunk_count, aux_count, part * aux_count)

    before = None
    if chunk_count > 1:
        before = apply_metric(after(products[:-1], made), metric, 0, None, jnp.float32)
    result = apply_metric(products[-1:], metric, chunk_count - 1, before, jnp.bfloat16)
    return result.reshape(group, domain // aux_count, part * aux_count)


def solution(mesh):
    in_specs = (
        P("orb", None, "aux"),
        P("orb", None, None, None),
        P("orb", None),
        P("aux", None, None),
        P("aux", None),
    )
    body = functools.partial(shards, mesh.shape["orb"], mesh.shape["aux"])
    return jax.shard_map(body, mesh=mesh, in_specs=in_specs, out_specs=P("orb", "aux", None), check_vma=False)
```

```python
import functools

import jax
import jax.numpy as jnp
from jax import lax
from jax.experimental import pallas as pl
from jax.experimental.pallas import tpu as pltpu
from jax.sharding import PartitionSpec as P

VMEM_LIMIT = 40 * 1024 * 1024
VMEM_WHOLE = 58 * 1024 * 1024


def largest_divisor(total, most):
    return max(size for size in range(1, most + 1) if total % size == 0)


def pack_kernel(width, source, *chunks):
    half = source.shape[1] // 2
    for at, chunk in enumerate(chunks):
        columns = slice(at * width, (at + 1) * width)
        chunk[...] = jnp.concatenate([source[:, :half, columns], source[:, half:, columns]], axis=-1)


def pack_chunks(factors, width):
    orbitals, domain, part = factors.shape
    count = part // width
    step = largest_divisor(orbitals, 12)
    packed = (step, domain // 2, 2 * width)
    return pl.pallas_call(
        functools.partial(pack_kernel, width),
        grid=(orbitals // step,),
        in_specs=[pl.BlockSpec((step, domain, part), lambda i: (i, 0, 0))],
        out_specs=[pl.BlockSpec(packed, lambda i: (i, 0, 0))] * count,
        out_shape=[jax.ShapeDtypeStruct((orbitals,) + packed[1:], factors.dtype)] * count,
        cost_estimate=pl.CostEstimate(flops=0, bytes_accessed=4 * factors.size, transcendentals=0),
        compiler_params=pltpu.CompilerParams(vmem_limit_bytes=VMEM_WHOLE),
        name="pack_chunks",
    )(factors)


def halves_apart(one, two, half):
    lower = jnp.concatenate([one[:, :half], two[:, :half]], axis=1)
    upper = jnp.concatenate([one[:, half:], two[:, half:]], axis=1)
    return lower, upper


def product_kernel(pairs, split_rows, slots, amplitudes, *refs):
    pieces = refs[:-3]
    out, table, arrived = refs[-3:]
    group, half_domain, lanes = pieces[0].shape
    here = pl.program_id(0)

    @pl.when(here == 0)
    def _():
        copies = [
            pltpu.make_async_copy(piece, table.at[pl.ds(at * group, group)], arrived.at[at])
            for at, piece in enumerate(pieces)
        ]
        for copy in copies:
            copy.start()
        for copy in copies:
            copy.wait()

    step, domain = amplitudes.shape[1], amplitudes.shape[3]
    half_count = pl.num_programs(0) * step
    first = lax.broadcasted_iota(jnp.int32, (domain, lanes), 1) < lanes // 2
    for q in range(step):
        sums = []
        for side in range(2):
            base = (side * half_count + here * step + q) * pairs
            lower, upper = [], []
            for k in range(0, pairs, 2):
                low, high = halves_apart(amplitudes[side, q, k], amplitudes[side, q, k + 1], half_domain)
                lower.append(low)
                upper.append(high)
            left = jnp.concatenate([jnp.concatenate(lower, axis=1), jnp.concatenate(upper, axis=1)], axis=0)
            right = jnp.concatenate([table[slots[base + k]] for k in range(pairs)], axis=0)
            sums.append(jnp.dot(left, right, preferred_element_type=jnp.float32))
        placed = jnp.where(first, sums[0][:domain], sums[1][domain:])
        moved = jnp.where(first, sums[1][:domain], sums[0][domain:])
        both = (placed + pltpu.roll(moved, lanes // 2, 1)).astype(out.dtype)
        if split_rows:
            owners, rows = out.shape[0], domain // out.shape[0]
            out[:, q * rows : (q + 1) * rows, :] = both.reshape(owners, rows, lanes)
        else:
            out[q] = both


def chunk_products(slots, amplitudes, pieces, owners):
    orbitals, pairs, domain, _ = amplitudes.shape
    group, half_domain, lanes = pieces[0].shape
    total = group * len(pieces)
    half = orbitals // 2
    rows = domain // owners
    split_rows = rows % 16 == 0
    step = largest_divisor(half, 4)
    if split_rows:
        out_shape, out_block, out_at = (owners, half * rows, lanes), (owners, step * rows, lanes), lambda i, s: (0, i, 0)
    else:
        out_shape, out_block, out_at = (half, domain, lanes), (step, domain, lanes), lambda i, s: (i, 0, 0)
    result = pl.pallas_call(
        functools.partial(product_kernel, pairs, split_rows),
        grid_spec=pltpu.PrefetchScalarGridSpec(
            num_scalar_prefetch=1,
            grid=(half // step,),
            in_specs=[pl.BlockSpec((2, step, pairs, domain, domain), lambda i, s: (0, i, 0, 0, 0))]
            + [pl.BlockSpec(memory_space=pl.ANY)] * len(pieces),
            out_specs=pl.BlockSpec(out_block, out_at),
            scratch_shapes=[
                pltpu.VMEM((total, half_domain, lanes), jnp.bfloat16),
                pltpu.SemaphoreType.DMA((len(pieces),)),
            ],
        ),
        out_shape=jax.ShapeDtypeStruct(out_shape, jnp.bfloat16),
        cost_estimate=pl.CostEstimate(
            flops=8 * amplitudes.size * lanes,
            bytes_accessed=2 * amplitudes.size + 2 * total * half_domain * lanes,
            transcendentals=0,
        ),
        compiler_params=pltpu.CompilerParams(vmem_limit_bytes=VMEM_LIMIT),
        name="chunk_products",
    )(slots, amplitudes.reshape(2, half, pairs, domain, domain), *pieces)
    if split_rows:
        return result
    result = result.reshape(half, owners, rows, lanes).transpose(1, 0, 2, 3)
    return result.reshape(owners, half * rows, lanes)


def join_kernel(*refs):
    for at, piece in enumerate(refs[:-1]):
        refs[-1][at] = piece[...]


def join(pieces):
    shape = (len(pieces),) + pieces[0].shape
    return pl.pallas_call(
        join_kernel,
        out_shape=jax.ShapeDtypeStruct(shape, pieces[0].dtype),
        cost_estimate=pl.CostEstimate(flops=0, bytes_accessed=4 * len(pieces) * pieces[0].size, transcendentals=0),
        compiler_params=pltpu.CompilerParams(vmem_limit_bytes=VMEM_LIMIT),
        name="join",
    )(*pieces)


def place_kernel(chunks, owners, tiles_each, positions, *refs):
    sources, out = refs[:-1], refs[-1]
    devices, _, span = sources[0].shape
    width = span // 2
    out[...] = jnp.zeros_like(out)
    for which, source in enumerate(sources):

        @pl.loop(0, devices)
        def _(device):
            for at in range(tiles_each):
                number = (which * devices + device) * tiles_each + at
                column = pl.multiple_of(positions[2 * number + 1] * span, span)
                for side in range(2):
                    block = 2 * positions[2 * number] + side
                    row = ((block % chunks) * owners + block // chunks) * width
                    begin = at * span + side * width
                    out[pl.ds(pl.multiple_of(row, width), width), pl.ds(column, span)] = source[
                        device, begin : begin + width, :
                    ]


def place_tiles(positions, sources, tiles_each, chunks, owners, size):
    shape = sources[0].shape
    return pl.pallas_call(
        functools.partial(place_kernel, chunks, owners, tiles_each),
        grid_spec=pltpu.PrefetchScalarGridSpec(
            num_scalar_prefetch=1,
            grid=(1,),
            in_specs=[pl.BlockSpec(shape, lambda i, s: (0, 0, 0))] * len(sources),
            out_specs=pl.BlockSpec((size, size), lambda i, s: (0, 0)),
        ),
        out_shape=jax.ShapeDtypeStruct((size, size), sources[0].dtype),
        cost_estimate=pl.CostEstimate(
            flops=0, bytes_accessed=2 * len(sources) * sources[0].size + 2 * size * size, transcendentals=0
        ),
        compiler_params=pltpu.CompilerParams(vmem_limit_bytes=VMEM_LIMIT),
        name="place_tiles",
    )(positions, *sources)


def metric_kernel(count, has_before, *refs):
    chunks, metric, before = refs[:count], refs[count], refs[count + 1]
    out, rows = refs[-2:]
    owners, height, lanes = chunks[0].shape
    width = lanes // 2

    @pl.when(pl.program_id(0) == 0)
    def _():
        for at, chunk in enumerate(chunks):
            for owner in range(0, owners, 2):
                one, two = chunk[owner], chunk[owner + 1]
                columns = pl.ds((at * owners + owner) * width, lanes)
                rows[:height, columns] = jnp.concatenate([one[:, :width], two[:, :width]], axis=1)
                rows[height:, columns] = jnp.concatenate([one[:, width:], two[:, width:]], axis=1)

    for side in range(2):
        sums = jnp.dot(rows[side * height : (side + 1) * height], metric[...], preferred_element_type=jnp.float32)
        if has_before:
            sums += before[side]
        out[side] = sums.astype(out.dtype)


def apply_metric(chunks, metric, begin, before, dtype):
    owners, height, lanes = chunks[0].shape
    size = metric.shape[0]
    depth = len(chunks) * owners * lanes // 2
    step = largest_divisor(size, 256)
    sums = [] if before is None else [before]
    block = pl.BlockSpec((2, height, step), lambda j: (0, 0, j))
    return pl.pallas_call(
        functools.partial(metric_kernel, len(chunks), before is not None),
        grid=(size // step,),
        in_specs=[pl.BlockSpec((owners, height, lanes), lambda j: (0, 0, 0))] * len(chunks)
        + [pl.BlockSpec((depth, step), lambda j: (begin // len(chunks), j))]
        + [block] * len(sums),
        out_specs=block,
        out_shape=jax.ShapeDtypeStruct((2, height, size), dtype),
        scratch_shapes=[pltpu.VMEM((2 * height, depth), jnp.bfloat16)],
        cost_estimate=pl.CostEstimate(
            flops=4 * height * depth * size,
            bytes_accessed=2 * depth * size + 12 * height * size,
            transcendentals=0,
        ),
        compiler_params=pltpu.CompilerParams(vmem_limit_bytes=VMEM_WHOLE),
        name="apply_metric",
    )(*chunks, metric, *sums)


def after(value, others):
    return lax.optimization_barrier((value, others))[0]


def shards(orb_count, aux_count, factors, amplitudes, partners, metric_tiles, tile_pos):
    group, domain, part = factors.shape
    span = metric_tiles.shape[1]
    width = span // 2
    chunk_count = part // width
    far_count = orb_count // 2
    me = lax.axis_index("orb")

    def to_far(array, shift):
        moves = [(g, (g + 2 * shift) % orb_count) for g in range(orb_count)]
        return lax.ppermute(array, "orb", moves)

    def to_mate(array):
        return lax.ppermute(array, "orb", [(g, g ^ 1) for g in range(orb_count)])

    owner, place = partners // group, partners % group
    far = (me // 2 - owner // 2) % far_count
    slots = ((far * 2 + (me % 2 + owner) % 2) * group + place).reshape(-1)

    half_tiles = metric_tiles.shape[0] // 2
    mine = (me % 2) * half_tiles
    tiles = lax.dynamic_slice_in_dim(metric_tiles, mine, half_tiles, axis=0).reshape(half_tiles * span, span)
    spots = lax.dynamic_slice_in_dim(tile_pos, mine, half_tiles, axis=0).reshape(-1).astype(tiles.dtype)
    spot_rows = -(-spots.size // (16 * span)) * 16
    spots = jnp.pad(spots, (0, spot_rows * span - spots.size)).reshape(spot_rows, span)
    load = jnp.concatenate([tiles, spots], axis=0)
    parts = [load]
    for shift in range(1, aux_count // 2):
        moves = [(g, (g + 2 * shift) % aux_count) for g in range(aux_count)]
        parts.append(lax.ppermute(load, "aux", moves))

    column = join(parts)
    beside = lax.ppermute(column, "aux", [(g, g ^ 1) for g in range(aux_count)])
    sources = [column, beside, to_mate(column), to_mate(beside)]

    packed = pack_chunks(factors, width)
    before_far = {1: parts[1::2]}
    before_rows = {0: parts, 1: beside, 2: sources[2:]}
    products = []
    far_pieces, made = [], None
    for at in range(chunk_count):
        own = packed[at]
        if at:
            own = after(own, [far_pieces, before_far.get(at, [])])
        far_pieces = [to_far(own, shift) for shift in range(1, far_count)]
        if at:
            far_pieces = after(far_pieces, made)
        pieces = []
        for piece in [packed[at]] + far_pieces:
            pieces += [piece, to_mate(piece)]
        made = chunk_products(slots, amplitudes, pieces, aux_count)
        rows = after(made, before_rows[at]) if at in before_rows and chunk_count > 1 else made
        products.append(lax.all_to_all(rows, "aux", split_axis=0, concat_axis=0, tiled=True))

    positions = jnp.concatenate([source[:, half_tiles * span, : 2 * half_tiles] for source in sources])
    positions = positions.astype(jnp.int32).reshape(-1)
    metric = place_tiles(positions, sources, half_tiles, chunk_count, aux_count, part * aux_count)

    before = None
    if chunk_count > 1:
        before = apply_metric(after(products[:-1], made), metric, 0, None, jnp.float32)
    result = apply_metric(products[-1:], metric, chunk_count - 1, before, jnp.bfloat16)
    return result.reshape(group, domain // aux_count, part * aux_count)


def solution(mesh):
    in_specs = (
        P("orb", None, "aux"),
        P("orb", None, None, None),
        P("orb", None),
        P("aux", None, None),
        P("aux", None),
    )
    body = functools.partial(shards, mesh.shape["orb"], mesh.shape["aux"])
    return jax.shard_map(body, mesh=mesh, in_specs=in_specs, out_specs=P("orb", "aux", None), check_vma=False)
```

```python
import functools

import jax
import jax.numpy as jnp
from jax import lax
from jax.experimental import pallas as pl
from jax.experimental.pallas import tpu as pltpu
from jax.sharding import PartitionSpec as P

VMEM_LIMIT = 40 * 1024 * 1024
VMEM_WHOLE = 58 * 1024 * 1024


def largest_divisor(total, most):
    return max(size for size in range(1, most + 1) if total % size == 0)


def pack_kernel(width, first, source, *chunks):
    half = source.shape[1] // 2
    for at, chunk in enumerate(chunks):
        columns = slice(first + at * width, first + (at + 1) * width)
        chunk[...] = jnp.concatenate([source[:, :half, columns], source[:, half:, columns]], axis=-1)


def pack_chunks(factors, width, begin, count, cost):
    orbitals, domain, part = factors.shape
    first = begin * width
    step = largest_divisor(orbitals, 12)
    packed = (step, domain // 2, 2 * width)
    return pl.pallas_call(
        functools.partial(pack_kernel, width, first),
        grid=(orbitals // step,),
        in_specs=[pl.BlockSpec((step, domain, part), lambda i: (i, 0, 0))],
        out_specs=[pl.BlockSpec(packed, lambda i: (i, 0, 0))] * count,
        out_shape=[jax.ShapeDtypeStruct((orbitals,) + packed[1:], factors.dtype)] * count,
        cost_estimate=pl.CostEstimate(flops=0, bytes_accessed=cost * factors.size, transcendentals=0),
        compiler_params=pltpu.CompilerParams(vmem_limit_bytes=VMEM_WHOLE),
        name="pack_chunks",
    )(factors)


def halves_apart(one, two, half):
    lower = jnp.concatenate([one[:, :half], two[:, :half]], axis=1)
    upper = jnp.concatenate([one[:, half:], two[:, half:]], axis=1)
    return lower, upper


def product_kernel(pairs, split_rows, streams, slots, *refs):
    amplitudes, pieces = refs[: 2 * streams], refs[2 * streams : -3]
    out, table, arrived = refs[-3:]
    group, half_domain, lanes = pieces[0].shape
    here = pl.program_id(0)

    @pl.when(here == 0)
    def _():
        copies = [
            pltpu.make_async_copy(piece, table.at[pl.ds(at * group, group)], arrived.at[at])
            for at, piece in enumerate(pieces)
        ]
        for copy in copies:
            copy.start()
        for copy in copies:
            copy.wait()

    step, domain = amplitudes[0].shape[1], amplitudes[0].shape[3]
    each = pairs // streams
    half_count = pl.num_programs(0) * step
    first = lax.broadcasted_iota(jnp.int32, (domain, lanes), 1) < lanes // 2
    for q in range(step):
        sums = []
        for side in range(2):
            base = (side * half_count + here * step + q) * pairs
            lower, upper = [], []
            for k in range(0, pairs, 2):
                tiles = amplitudes[side * streams + k // each]
                low, high = halves_apart(tiles[0, q, k % each], tiles[0, q, k % each + 1], half_domain)
                lower.append(low)
                upper.append(high)
            left = jnp.concatenate([jnp.concatenate(lower, axis=1), jnp.concatenate(upper, axis=1)], axis=0)
            right = jnp.concatenate([table[slots[base + k]] for k in range(pairs)], axis=0)
            sums.append(jnp.dot(left, right, preferred_element_type=jnp.float32))
        placed = jnp.where(first, sums[0][:domain], sums[1][domain:])
        moved = jnp.where(first, sums[1][:domain], sums[0][domain:])
        both = (placed + pltpu.roll(moved, lanes // 2, 1)).astype(out.dtype)
        if split_rows:
            owners, rows = out.shape[0], domain // out.shape[0]
            out[:, q * rows : (q + 1) * rows, :] = both.reshape(owners, rows, lanes)
        else:
            out[q] = both


def chunk_products(slots, amplitudes, pieces, owners):
    orbitals, pairs, domain, _ = amplitudes.shape
    group, half_domain, lanes = pieces[0].shape
    total = group * len(pieces)
    half = orbitals // 2
    rows = domain // owners
    split_rows = rows % 16 == 0
    step = largest_divisor(half, 4)
    streams = 2 if pairs % 4 == 0 else 1
    tiles = (1, step, pairs // streams, domain, domain)
    if split_rows:
        out_shape, out_block, out_at = (owners, half * rows, lanes), (owners, step * rows, lanes), lambda i, s: (0, i, 0)
    else:
        out_shape, out_block, out_at = (half, domain, lanes), (step, domain, lanes), lambda i, s: (i, 0, 0)
    result = pl.pallas_call(
        functools.partial(product_kernel, pairs, split_rows, streams),
        grid_spec=pltpu.PrefetchScalarGridSpec(
            num_scalar_prefetch=1,
            grid=(half // step,),
            in_specs=[
                pl.BlockSpec(tiles, lambda i, s, side=side, part=part: (side, i, part, 0, 0))
                for side in range(2)
                for part in range(streams)
            ]
            + [pl.BlockSpec(memory_space=pl.ANY)] * len(pieces),
            out_specs=pl.BlockSpec(out_block, out_at),
            scratch_shapes=[
                pltpu.VMEM((total, half_domain, lanes), jnp.bfloat16),
                pltpu.SemaphoreType.DMA((len(pieces),)),
            ],
        ),
        out_shape=jax.ShapeDtypeStruct(out_shape, jnp.bfloat16),
        cost_estimate=pl.CostEstimate(
            flops=8 * amplitudes.size * lanes,
            bytes_accessed=2 * amplitudes.size + 2 * total * half_domain * lanes,
            transcendentals=0,
        ),
        compiler_params=pltpu.CompilerParams(vmem_limit_bytes=VMEM_LIMIT),
        name="chunk_products",
    )(slots, *[amplitudes.reshape(2, half, pairs, domain, domain)] * (2 * streams), *pieces)
    if split_rows:
        return result
    result = result.reshape(half, owners, rows, lanes).transpose(1, 0, 2, 3)
    return result.reshape(owners, half * rows, lanes)


def join_kernel(*refs):
    for at, piece in enumerate(refs[:-1]):
        refs[-1][at] = piece[...]


def join(pieces):
    shape = (len(pieces),) + pieces[0].shape
    return pl.pallas_call(
        join_kernel,
        out_shape=jax.ShapeDtypeStruct(shape, pieces[0].dtype),
        cost_estimate=pl.CostEstimate(flops=0, bytes_accessed=4 * len(pieces) * pieces[0].size, transcendentals=0),
        compiler_params=pltpu.CompilerParams(vmem_limit_bytes=VMEM_LIMIT),
        name="join",
    )(*pieces)


def place_tiles(chunks, owners, tiles_each, positions, sources, dense):
    devices, _, span = sources[0].shape
    width = span // 2
    dense[...] = jnp.zeros_like(dense)
    for which, source in enumerate(sources):

        @pl.loop(0, devices)
        def _(device):
            for at in range(tiles_each):
                number = (which * devices + device) * tiles_each + at
                column = pl.multiple_of(positions[2 * number + 1] * span, span)
                for side in range(2):
                    block = 2 * positions[2 * number] + side
                    row = ((block % chunks) * owners + block // chunks) * width
                    begin = at * span + side * width
                    dense[pl.ds(pl.multiple_of(row, width), width), pl.ds(column, span)] = source[
                        device, begin : begin + width, :
                    ]


def unpack_rows(chunks, rows):
    owners, height, lanes = chunks[0].shape
    width = lanes // 2
    for at, chunk in enumerate(chunks):
        for owner in range(0, owners, 2):
            one, two = chunk[owner], chunk[owner + 1]
            columns = pl.ds((at * owners + owner) * width, lanes)
            rows[:height, columns] = jnp.concatenate([one[:, :width], two[:, :width]], axis=1)
            rows[height:, columns] = jnp.concatenate([one[:, width:], two[:, width:]], axis=1)


def first_kernel(count, source_count, tiles_each, positions, *refs):
    chunks, sources = refs[:count], refs[count : count + source_count]
    *outs, dense, rows = refs[count + source_count :]
    owners, height, _ = chunks[0].shape
    depth = rows.shape[1]

    @pl.when(pl.program_id(0) == 0)
    def _():
        place_tiles(dense.shape[0] // (depth // count), owners, tiles_each, positions, sources, dense)
        unpack_rows(chunks, rows)

    step = outs[0].shape[-1]
    columns = pl.ds(pl.multiple_of(pl.program_id(0) * step, step), step)
    if len(outs) > 2:
        outs[2][...] = dense[depth:, columns]
    for side in range(2):
        part = rows[side * height : (side + 1) * height]
        sums = jnp.dot(part, dense[:depth, columns], preferred_element_type=jnp.float32)
        outs[side][...] = sums.astype(outs[side].dtype)


def first_shares(chunks, positions, sources, tiles_each, size, dtype):
    owners, height, lanes = chunks[0].shape
    depth = len(chunks) * owners * lanes // 2
    step = largest_divisor(size, 256)
    whole = lambda j, s: (0, 0, 0)
    heights = [height] * 2 + ([size - depth] if depth < size else [])
    kinds = [dtype] * 2 + [sources[0].dtype]
    return pl.pallas_call(
        functools.partial(first_kernel, len(chunks), len(sources), tiles_each),
        grid_spec=pltpu.PrefetchScalarGridSpec(
            num_scalar_prefetch=1,
            grid=(size // step,),
            in_specs=[pl.BlockSpec(array.shape, whole) for array in [*chunks, *sources]],
            out_specs=[pl.BlockSpec((tall, step), lambda j, s: (0, j)) for tall in heights],
            scratch_shapes=[
                pltpu.VMEM((size, size), sources[0].dtype),
                pltpu.VMEM((2 * height, depth), jnp.bfloat16),
            ],
        ),
        out_shape=[jax.ShapeDtypeStruct((tall, size), kind) for tall, kind in zip(heights, kinds)],
        cost_estimate=pl.CostEstimate(
            flops=4 * height * depth * size,
            bytes_accessed=2 * depth * size + 8 * height * size,
            transcendentals=0,
        ),
        compiler_params=pltpu.CompilerParams(vmem_limit_bytes=VMEM_WHOLE),
        name="first_shares",
    )(positions, *chunks, *sources)


def last_kernel(chunk, metric, one, two, out, rows):
    height = chunk.shape[1]

    @pl.when(pl.program_id(0) == 0)
    def _():
        unpack_rows([chunk], rows)

    for side, before in enumerate((one, two)):
        part = rows[side * height : (side + 1) * height]
        sums = jnp.dot(part, metric[...], preferred_element_type=jnp.float32)
        out[side] = (sums + before[...]).astype(out.dtype)


def last_share(chunk, metric, one, two):
    owners, height, lanes = chunk.shape
    depth, size = metric.shape
    step = largest_divisor(size, 256)
    tall = pl.BlockSpec((height, step), lambda j: (0, j))
    return pl.pallas_call(
        last_kernel,
        grid=(size // step,),
        in_specs=[
            pl.BlockSpec(chunk.shape, lambda j: (0, 0, 0)),
            pl.BlockSpec((depth, step), lambda j: (0, j)),
            tall,
            tall,
        ],
        out_specs=pl.BlockSpec((2, height, step), lambda j: (0, 0, j)),
        out_shape=jax.ShapeDtypeStruct((2, height, size), jnp.bfloat16),
        scratch_shapes=[pltpu.VMEM((2 * height, depth), jnp.bfloat16)],
        cost_estimate=pl.CostEstimate(
            flops=4 * height * depth * size,
            bytes_accessed=2 * depth * size + 12 * height * size,
            transcendentals=0,
        ),
        compiler_params=pltpu.CompilerParams(vmem_limit_bytes=VMEM_WHOLE),
        name="last_share",
    )(chunk, metric, one, two)


def after(value, others):
    return lax.optimization_barrier((value, others))[0]


def shards(orb_count, aux_count, factors, amplitudes, partners, metric_tiles, tile_pos):
    group, domain, part = factors.shape
    span = metric_tiles.shape[1]
    width = span // 2
    chunk_count = part // width
    far_count = orb_count // 2
    me = lax.axis_index("orb")

    def to_far(array, shift):
        moves = [(g, (g + 2 * shift) % orb_count) for g in range(orb_count)]
        return lax.ppermute(array, "orb", moves)

    def to_mate(array):
        return lax.ppermute(array, "orb", [(g, g ^ 1) for g in range(orb_count)])

    owner, place = partners // group, partners % group
    far = (me // 2 - owner // 2) % far_count
    slots = ((far * 2 + (me % 2 + owner) % 2) * group + place).reshape(-1)

    half_tiles = metric_tiles.shape[0] // 2
    mine = (me % 2) * half_tiles
    tiles = lax.dynamic_slice_in_dim(metric_tiles, mine, half_tiles, axis=0).reshape(half_tiles * span, span)
    spots = lax.dynamic_slice_in_dim(tile_pos, mine, half_tiles, axis=0).reshape(-1).astype(tiles.dtype)
    spot_rows = -(-spots.size // (16 * span)) * 16
    spots = jnp.pad(spots, (0, spot_rows * span - spots.size)).reshape(spot_rows, span)
    load = jnp.concatenate([tiles, spots], axis=0)
    parts = [load]
    for shift in range(1, aux_count // 2):
        moves = [(g, (g + 2 * shift) % aux_count) for g in range(aux_count)]
        parts.append(lax.ppermute(load, "aux", moves))

    packed = list(pack_chunks(factors, width, 0, 1, 2))
    if chunk_count > 1:
        packed += pack_chunks(factors, width, 1, chunk_count - 1, 40)
        parts = after(parts, packed[1:])

    column = join(parts)
    beside = lax.ppermute(column, "aux", [(g, g ^ 1) for g in range(aux_count)])
    sources = [column, beside, to_mate(column), to_mate(beside)]

    before_far = {1: parts}
    before_products = {1: beside, 2: sources[2:]}
    products = []
    far_pieces, made = [], None
    for at in range(chunk_count):
        own = packed[at]
        if at:
            own = after(own, [far_pieces, before_far.get(at, [])])
        far_pieces = [to_far(own, shift) for shift in range(1, far_count)]
        if chunk_count > 1:
            far_pieces = after(far_pieces, made if at else packed[1:])
        pieces = []
        for piece in [packed[at]] + far_pieces:
            pieces += [piece, to_mate(piece)]
        places = after(slots, before_products[at]) if at in before_products else slots
        made = chunk_products(places, amplitudes, pieces, aux_count)
        products.append(lax.all_to_all(made, "aux", split_axis=0, concat_axis=0, tiled=True))

    positions = jnp.concatenate([source[:, half_tiles * span, : 2 * half_tiles] for source in sources])
    positions = positions.astype(jnp.int32).reshape(-1)
    size = part * aux_count
    if chunk_count > 1:
        ready = after(products[:-1], made)
        one, two, metric = first_shares(ready, positions, sources, half_tiles, size, jnp.float32)
        result = last_share(products[-1], metric, one, two)
    else:
        result = jnp.stack(first_shares(products, positions, sources, half_tiles, size, jnp.bfloat16))
    return result.reshape(group, domain // aux_count, size)


def solution(mesh):
    in_specs = (
        P("orb", None, "aux"),
        P("orb", None, None, None),
        P("orb", None),
        P("aux", None, None),
        P("aux", None),
    )
    body = functools.partial(shards, mesh.shape["orb"], mesh.shape["aux"])
    return jax.shard_map(body, mesh=mesh, in_specs=in_specs, out_specs=P("orb", "aux", None), check_vma=False)
```

```python
import functools

import jax
import jax.numpy as jnp
from jax import lax
from jax.experimental import pallas as pl
from jax.experimental.pallas import tpu as pltpu
from jax.sharding import PartitionSpec as P

VMEM_WHOLE = 58 * 1024 * 1024
SMALL = pl.CostEstimate(flops=0, bytes_accessed=4096, transcendentals=0)


def largest_divisor(total, most):
    return max(size for size in range(1, most + 1) if total % size == 0)


def pack_kernel(width, first, source, *chunks):
    half = source.shape[1] // 2
    for at, chunk in enumerate(chunks):
        columns = slice(first + at * width, first + (at + 1) * width)
        chunk[...] = jnp.concatenate([source[:, :half, columns], source[:, half:, columns]], axis=-1)


def pack_chunks(factors, width, begin, count):
    orbitals, domain, part = factors.shape
    first = begin * width
    step = largest_divisor(orbitals, 12)
    packed = (step, domain // 2, 2 * width)
    return pl.pallas_call(
        functools.partial(pack_kernel, width, first),
        grid=(orbitals // step,),
        in_specs=[pl.BlockSpec((step, domain, part), lambda i: (i, 0, 0))],
        out_specs=[pl.BlockSpec(packed, lambda i: (i, 0, 0))] * count,
        out_shape=[jax.ShapeDtypeStruct((orbitals,) + packed[1:], factors.dtype)] * count,
        cost_estimate=SMALL,
        compiler_params=pltpu.CompilerParams(vmem_limit_bytes=VMEM_WHOLE),
        name="pack_chunks",
    )(factors)


def halves_apart(one, two, half):
    lower = jnp.concatenate([one[:, :half], two[:, :half]], axis=1)
    upper = jnp.concatenate([one[:, half:], two[:, half:]], axis=1)
    return lower, upper


def product_kernel(pairs, split_rows, streams, slots, *refs):
    amplitudes, pieces = refs[: 2 * streams], refs[2 * streams : -3]
    out, table, arrived = refs[-3:]
    group, half_domain, lanes = pieces[0].shape
    here = pl.program_id(0)

    @pl.when(here == 0)
    def _():
        copies = [
            pltpu.make_async_copy(piece, table.at[pl.ds(at * group, group)], arrived.at[at])
            for at, piece in enumerate(pieces)
        ]
        for copy in copies:
            copy.start()
        for copy in copies:
            copy.wait()

    step, domain = amplitudes[0].shape[1], amplitudes[0].shape[3]
    each = pairs // streams
    half_count = pl.num_programs(0) * step
    first = lax.broadcasted_iota(jnp.int32, (domain, lanes), 1) < lanes // 2
    for q in range(step):
        sums = []
        for side in range(2):
            base = (side * half_count + here * step + q) * pairs
            lower, upper = [], []
            for k in range(0, pairs, 2):
                tiles = amplitudes[side * streams + k // each]
                low, high = halves_apart(tiles[0, q, k % each], tiles[0, q, k % each + 1], half_domain)
                lower.append(low)
                upper.append(high)
            left = jnp.concatenate([jnp.concatenate(lower, axis=1), jnp.concatenate(upper, axis=1)], axis=0)
            right = jnp.concatenate([table[slots[base + k]] for k in range(pairs)], axis=0)
            sums.append(jnp.dot(left, right, preferred_element_type=jnp.float32))
        placed = jnp.where(first, sums[0][:domain], sums[1][domain:])
        moved = jnp.where(first, sums[1][:domain], sums[0][domain:])
        both = (placed + pltpu.roll(moved, lanes // 2, 1)).astype(out.dtype)
        if split_rows:
            owners, rows = out.shape[0], domain // out.shape[0]
            out[:, q * rows : (q + 1) * rows, :] = both.reshape(owners, rows, lanes)
        else:
            out[q] = both


def chunk_products(slots, amplitudes, pieces, owners):
    orbitals, pairs, domain, _ = amplitudes.shape
    group, half_domain, lanes = pieces[0].shape
    total = group * len(pieces)
    half = orbitals // 2
    rows = domain // owners
    split_rows = rows % 16 == 0
    step = largest_divisor(half, 4)
    streams = 2 if pairs % 4 == 0 else 1
    tiles = (1, step, pairs // streams, domain, domain)
    if split_rows:
        out_shape, out_block, out_at = (owners, half * rows, lanes), (owners, step * rows, lanes), lambda i, s: (0, i, 0)
    else:
        out_shape, out_block, out_at = (half, domain, lanes), (step, domain, lanes), lambda i, s: (i, 0, 0)
    result = pl.pallas_call(
        functools.partial(product_kernel, pairs, split_rows, streams),
        grid_spec=pltpu.PrefetchScalarGridSpec(
            num_scalar_prefetch=1,
            grid=(half // step,),
            in_specs=[
                pl.BlockSpec(tiles, lambda i, s, side=side, part=part: (side, i, part, 0, 0))
                for side in range(2)
                for part in range(streams)
            ]
            + [pl.BlockSpec(memory_space=pl.ANY)] * len(pieces),
            out_specs=pl.BlockSpec(out_block, out_at),
            scratch_shapes=[
                pltpu.VMEM((total, half_domain, lanes), jnp.bfloat16),
                pltpu.SemaphoreType.DMA((len(pieces),)),
            ],
        ),
        out_shape=jax.ShapeDtypeStruct(out_shape, jnp.bfloat16),
        cost_estimate=SMALL,
        compiler_params=pltpu.CompilerParams(vmem_limit_bytes=VMEM_WHOLE),
        name="chunk_products",
    )(slots, *[amplitudes.reshape(2, half, pairs, domain, domain)] * (2 * streams), *pieces)
    if split_rows:
        return result
    result = result.reshape(half, owners, rows, lanes).transpose(1, 0, 2, 3)
    return result.reshape(owners, half * rows, lanes)


def join_kernel(*refs):
    for at, piece in enumerate(refs[:-1]):
        refs[-1][at] = piece[...]


def join(pieces):
    shape = (len(pieces),) + pieces[0].shape
    return pl.pallas_call(
        join_kernel,
        out_shape=jax.ShapeDtypeStruct(shape, pieces[0].dtype),
        cost_estimate=SMALL,
        compiler_params=pltpu.CompilerParams(vmem_limit_bytes=VMEM_WHOLE),
        name="join",
    )(*pieces)


def place_tiles(chunks, owners, tiles_each, positions, sources, dense):
    devices, _, span = sources[0].shape
    width = span // 2
    dense[...] = jnp.zeros_like(dense)
    for which, source in enumerate(sources):

        @pl.loop(0, devices)
        def _(device):
            for at in range(tiles_each):
                number = (which * devices + device) * tiles_each + at
                column = pl.multiple_of(positions[2 * number + 1] * span, span)
                for side in range(2):
                    block = 2 * positions[2 * number] + side
                    row = ((block % chunks) * owners + block // chunks) * width
                    begin = at * span + side * width
                    dense[pl.ds(pl.multiple_of(row, width), width), pl.ds(column, span)] = source[
                        device, begin : begin + width, :
                    ]


def unpack_rows(chunks, rows):
    owners, height, lanes = chunks[0].shape
    width = lanes // 2
    for at, chunk in enumerate(chunks):
        for owner in range(0, owners, 2):
            one, two = chunk[owner], chunk[owner + 1]
            columns = pl.ds((at * owners + owner) * width, lanes)
            rows[:height, columns] = jnp.concatenate([one[:, :width], two[:, :width]], axis=1)
            rows[height:, columns] = jnp.concatenate([one[:, width:], two[:, width:]], axis=1)


def first_kernel(count, source_count, tiles_each, positions, *refs):
    chunks, sources = refs[:count], refs[count : count + source_count]
    *outs, dense, rows = refs[count + source_count :]
    owners, height, _ = chunks[0].shape
    depth = rows.shape[1]

    @pl.when(pl.program_id(0) == 0)
    def _():
        place_tiles(dense.shape[0] // (depth // count), owners, tiles_each, positions, sources, dense)
        unpack_rows(chunks, rows)

    step = outs[0].shape[-1]
    columns = pl.ds(pl.multiple_of(pl.program_id(0) * step, step), step)
    if len(outs) > 2:
        outs[2][...] = dense[depth:, columns]
    for side in range(2):
        part = rows[side * height : (side + 1) * height]
        sums = jnp.dot(part, dense[:depth, columns], preferred_element_type=jnp.float32)
        outs[side][...] = sums.astype(outs[side].dtype)


def first_shares(chunks, positions, sources, tiles_each, size, dtype):
    owners, height, lanes = chunks[0].shape
    depth = len(chunks) * owners * lanes // 2
    step = largest_divisor(size, 256)
    whole = lambda j, s: (0, 0, 0)
    heights = [height] * 2 + ([size - depth] if depth < size else [])
    kinds = [dtype] * 2 + [sources[0].dtype]
    return pl.pallas_call(
        functools.partial(first_kernel, len(chunks), len(sources), tiles_each),
        grid_spec=pltpu.PrefetchScalarGridSpec(
            num_scalar_prefetch=1,
            grid=(size // step,),
            in_specs=[pl.BlockSpec(array.shape, whole) for array in [*chunks, *sources]],
            out_specs=[pl.BlockSpec((tall, step), lambda j, s: (0, j)) for tall in heights],
            scratch_shapes=[
                pltpu.VMEM((size, size), sources[0].dtype),
                pltpu.VMEM((2 * height, depth), jnp.bfloat16),
            ],
        ),
        out_shape=[jax.ShapeDtypeStruct((tall, size), kind) for tall, kind in zip(heights, kinds)],
        cost_estimate=SMALL,
        compiler_params=pltpu.CompilerParams(vmem_limit_bytes=VMEM_WHOLE),
        name="first_shares",
    )(positions, *chunks, *sources)


def last_kernel(chunk, metric, one, two, out, rows):
    height = chunk.shape[1]

    @pl.when(pl.program_id(0) == 0)
    def _():
        unpack_rows([chunk], rows)

    for side, before in enumerate((one, two)):
        part = rows[side * height : (side + 1) * height]
        sums = jnp.dot(part, metric[...], preferred_element_type=jnp.float32)
        out[side] = (sums + before[...]).astype(out.dtype)


def last_share(chunk, metric, one, two):
    owners, height, lanes = chunk.shape
    depth, size = metric.shape
    step = largest_divisor(size, 256)
    tall = pl.BlockSpec((height, step), lambda j: (0, j))
    return pl.pallas_call(
        last_kernel,
        grid=(size // step,),
        in_specs=[
            pl.BlockSpec(chunk.shape, lambda j: (0, 0, 0)),
            pl.BlockSpec((depth, step), lambda j: (0, j)),
            tall,
            tall,
        ],
        out_specs=pl.BlockSpec((2, height, step), lambda j: (0, 0, j)),
        out_shape=jax.ShapeDtypeStruct((2, height, size), jnp.bfloat16),
        scratch_shapes=[pltpu.VMEM((2 * height, depth), jnp.bfloat16)],
        cost_estimate=SMALL,
        compiler_params=pltpu.CompilerParams(vmem_limit_bytes=VMEM_WHOLE),
        name="last_share",
    )(chunk, metric, one, two)


def after(value, others):
    return lax.optimization_barrier((value, others))[0]


def shards(orb_count, aux_count, factors, amplitudes, partners, metric_tiles, tile_pos):
    group, domain, part = factors.shape
    span = metric_tiles.shape[1]
    width = span // 2
    chunk_count = part // width
    far_count = orb_count // 2
    me = lax.axis_index("orb")

    def to_far(array, shift):
        moves = [(g, (g + 2 * shift) % orb_count) for g in range(orb_count)]
        return lax.ppermute(array, "orb", moves)

    def to_mate(array):
        return lax.ppermute(array, "orb", [(g, g ^ 1) for g in range(orb_count)])

    owner, place = partners // group, partners % group
    far = (me // 2 - owner // 2) % far_count
    slots = ((far * 2 + (me % 2 + owner) % 2) * group + place).reshape(-1)

    half_tiles = metric_tiles.shape[0] // 2
    mine = (me % 2) * half_tiles
    tiles = lax.dynamic_slice_in_dim(metric_tiles, mine, half_tiles, axis=0).reshape(half_tiles * span, span)
    spots = lax.dynamic_slice_in_dim(tile_pos, mine, half_tiles, axis=0).reshape(-1).astype(tiles.dtype)
    spot_rows = -(-spots.size // (16 * span)) * 16
    spots = jnp.pad(spots, (0, spot_rows * span - spots.size)).reshape(spot_rows, span)
    load = jnp.concatenate([tiles, spots], axis=0)
    parts = [load]
    for shift in range(1, aux_count // 2):
        moves = [(g, (g + 2 * shift) % aux_count) for g in range(aux_count)]
        parts.append(lax.ppermute(load, "aux", moves))

    packed = list(pack_chunks(factors, width, 0, 1))
    if chunk_count > 1:
        packed += pack_chunks(factors, width, 1, chunk_count - 1)
        parts = after(parts, packed[1:])

    column = join(parts)
    beside = lax.ppermute(column, "aux", [(g, g ^ 1) for g in range(aux_count)])
    sources = [column, beside, to_mate(column), to_mate(beside)]

    before_far = {1: parts}
    before_products = {1: beside, 2: sources[2:]}
    products = []
    far_pieces, made = [], None
    for at in range(chunk_count):
        own = packed[at]
        if at:
            own = after(own, [far_pieces, before_far.get(at, [])])
        far_pieces = [to_far(own, shift) for shift in range(1, far_count)]
        if chunk_count > 1:
            far_pieces = after(far_pieces, made if at else [packed[1:], column])
        pieces = []
        for piece in [packed[at]] + far_pieces:
            pieces += [piece, to_mate(piece)]
        places = after(slots, before_products[at]) if at in before_products else slots
        made = chunk_products(places, amplitudes, pieces, aux_count)
        products.append(lax.all_to_all(made, "aux", split_axis=0, concat_axis=0, tiled=True))

    positions = jnp.concatenate([source[:, half_tiles * span, : 2 * half_tiles] for source in sources])
    positions = positions.astype(jnp.int32).reshape(-1)
    size = part * aux_count
    if chunk_count > 1:
        ready = after(products[:-1], made)
        one, two, metric = first_shares(ready, positions, sources, half_tiles, size, jnp.float32)
        result = last_share(products[-1], metric, one, two)
    else:
        result = jnp.stack(first_shares(products, positions, sources, half_tiles, size, jnp.bfloat16))
    return result.reshape(group, domain // aux_count, size)


def solution(mesh):
    in_specs = (
        P("orb", None, "aux"),
        P("orb", None, None, None),
        P("orb", None),
        P("aux", None, None),
        P("aux", None),
    )
    body = functools.partial(shards, mesh.shape["orb"], mesh.shape["aux"])
    return jax.shard_map(body, mesh=mesh, in_specs=in_specs, out_specs=P("orb", "aux", None), check_vma=False)
```

```python
import functools

import jax
import jax.numpy as jnp
from jax import lax
from jax.experimental import pallas as pl
from jax.experimental.pallas import tpu as pltpu
from jax.sharding import PartitionSpec as P

VMEM_WHOLE = 58 * 1024 * 1024
VMEM_MOST = 36 * 1024 * 1024
VMEM_PART = 20 * 1024 * 1024
SMALL = pl.CostEstimate(flops=0, bytes_accessed=4096, transcendentals=0)


def largest_divisor(total, most):
    return max(size for size in range(1, most + 1) if total % size == 0)


def pack_kernel(width, first, source, *chunks):
    half = source.shape[1] // 2
    for at, chunk in enumerate(chunks):
        columns = slice(first + at * width, first + (at + 1) * width)
        chunk[...] = jnp.concatenate([source[:, :half, columns], source[:, half:, columns]], axis=-1)


def pack_chunks(factors, width, begin, count):
    orbitals, domain, part = factors.shape
    first = begin * width
    step = largest_divisor(orbitals, 12)
    packed = (step, domain // 2, 2 * width)
    return pl.pallas_call(
        functools.partial(pack_kernel, width, first),
        grid=(orbitals // step,),
        in_specs=[pl.BlockSpec((step, domain, part), lambda i: (i, 0, 0))],
        out_specs=[pl.BlockSpec(packed, lambda i: (i, 0, 0))] * count,
        out_shape=[jax.ShapeDtypeStruct((orbitals,) + packed[1:], factors.dtype)] * count,
        cost_estimate=SMALL,
        compiler_params=pltpu.CompilerParams(vmem_limit_bytes=VMEM_WHOLE),
        name="pack_chunks",
    )(factors)


def halves_apart(one, two, half):
    lower = jnp.concatenate([one[:, :half], two[:, :half]], axis=1)
    upper = jnp.concatenate([one[:, half:], two[:, half:]], axis=1)
    return lower, upper


def product_kernel(pairs, split_rows, streams, slots, *refs):
    amplitudes, pieces = refs[: 2 * streams], refs[2 * streams : -3]
    out, table, arrived = refs[-3:]
    group, half_domain, lanes = pieces[0].shape
    here = pl.program_id(0)

    @pl.when(here == 0)
    def _():
        copies = [
            pltpu.make_async_copy(piece, table.at[pl.ds(at * group, group)], arrived.at[at])
            for at, piece in enumerate(pieces)
        ]
        for copy in copies:
            copy.start()
        for copy in copies:
            copy.wait()

    step, domain = amplitudes[0].shape[1], amplitudes[0].shape[3]
    each = pairs // streams
    half_count = pl.num_programs(0) * step
    first = lax.broadcasted_iota(jnp.int32, (domain, lanes), 1) < lanes // 2
    for q in range(step):
        sums = []
        for side in range(2):
            base = (side * half_count + here * step + q) * pairs
            lower, upper = [], []
            for k in range(0, pairs, 2):
                tiles = amplitudes[side * streams + k // each]
                low, high = halves_apart(tiles[0, q, k % each], tiles[0, q, k % each + 1], half_domain)
                lower.append(low)
                upper.append(high)
            left = jnp.concatenate([jnp.concatenate(lower, axis=1), jnp.concatenate(upper, axis=1)], axis=0)
            right = jnp.concatenate([table[slots[base + k]] for k in range(pairs)], axis=0)
            sums.append(jnp.dot(left, right, preferred_element_type=jnp.float32))
        placed = jnp.where(first, sums[0][:domain], sums[1][domain:])
        moved = jnp.where(first, sums[1][:domain], sums[0][domain:])
        both = (placed + pltpu.roll(moved, lanes // 2, 1)).astype(out.dtype)
        if split_rows:
            owners, rows = out.shape[0], domain // out.shape[0]
            out[:, q * rows : (q + 1) * rows, :] = both.reshape(owners, rows, lanes)
        else:
            out[q] = both


def chunk_products(slots, amplitudes, pieces, owners):
    orbitals, pairs, domain, _ = amplitudes.shape
    group, half_domain, lanes = pieces[0].shape
    total = group * len(pieces)
    half = orbitals // 2
    rows = domain // owners
    split_rows = rows % 16 == 0
    step = largest_divisor(half, 4)
    streams = 2 if pairs % 4 == 0 else 1
    tiles = (1, step, pairs // streams, domain, domain)
    if split_rows:
        out_shape, out_block, out_at = (owners, half * rows, lanes), (owners, step * rows, lanes), lambda i, s: (0, i, 0)
    else:
        out_shape, out_block, out_at = (half, domain, lanes), (step, domain, lanes), lambda i, s: (i, 0, 0)
    result = pl.pallas_call(
        functools.partial(product_kernel, pairs, split_rows, streams),
        grid_spec=pltpu.PrefetchScalarGridSpec(
            num_scalar_prefetch=1,
            grid=(half // step,),
            in_specs=[
                pl.BlockSpec(tiles, lambda i, s, side=side, part=part: (side, i, part, 0, 0))
                for side in range(2)
                for part in range(streams)
            ]
            + [pl.BlockSpec(memory_space=pl.ANY)] * len(pieces),
            out_specs=pl.BlockSpec(out_block, out_at),
            scratch_shapes=[
                pltpu.VMEM((total, half_domain, lanes), jnp.bfloat16),
                pltpu.SemaphoreType.DMA((len(pieces),)),
            ],
        ),
        out_shape=jax.ShapeDtypeStruct(out_shape, jnp.bfloat16),
        cost_estimate=SMALL,
        compiler_params=pltpu.CompilerParams(vmem_limit_bytes=VMEM_PART),
        name="chunk_products",
    )(slots, *[amplitudes.reshape(2, half, pairs, domain, domain)] * (2 * streams), *pieces)
    if split_rows:
        return result
    result = result.reshape(half, owners, rows, lanes).transpose(1, 0, 2, 3)
    return result.reshape(owners, half * rows, lanes)


def join_kernel(*refs):
    for at, piece in enumerate(refs[:-1]):
        refs[-1][at] = piece[...]


def join(pieces):
    shape = (len(pieces),) + pieces[0].shape
    return pl.pallas_call(
        join_kernel,
        out_shape=jax.ShapeDtypeStruct(shape, pieces[0].dtype),
        cost_estimate=SMALL,
        compiler_params=pltpu.CompilerParams(vmem_limit_bytes=VMEM_PART),
        name="join",
    )(*pieces)


def place_tiles(chunks, owners, tiles_each, positions, sources, dense):
    devices, _, span = sources[0].shape
    width = span // 2
    dense[...] = jnp.zeros_like(dense)
    for which, source in enumerate(sources):

        @pl.loop(0, devices)
        def _(device):
            for at in range(tiles_each):
                number = (which * devices + device) * tiles_each + at
                column = pl.multiple_of(positions[2 * number + 1] * span, span)
                for side in range(2):
                    block = 2 * positions[2 * number] + side
                    row = ((block % chunks) * owners + block // chunks) * width
                    begin = at * span + side * width
                    dense[pl.ds(pl.multiple_of(row, width), width), pl.ds(column, span)] = source[
                        device, begin : begin + width, :
                    ]


def unpack_rows(chunks, rows):
    owners, height, lanes = chunks[0].shape
    width = lanes // 2
    for at, chunk in enumerate(chunks):
        for owner in range(0, owners, 2):
            one, two = chunk[owner], chunk[owner + 1]
            columns = pl.ds((at * owners + owner) * width, lanes)
            rows[:height, columns] = jnp.concatenate([one[:, :width], two[:, :width]], axis=1)
            rows[height:, columns] = jnp.concatenate([one[:, width:], two[:, width:]], axis=1)


def first_kernel(count, source_count, tiles_each, positions, *refs):
    chunks, sources = refs[:count], refs[count : count + source_count]
    *outs, dense, rows = refs[count + source_count :]
    owners, height, _ = chunks[0].shape
    depth = rows.shape[1]

    @pl.when(pl.program_id(0) == 0)
    def _():
        place_tiles(dense.shape[0] // (depth // count), owners, tiles_each, positions, sources, dense)
        unpack_rows(chunks, rows)

    step = outs[0].shape[-1]
    columns = pl.ds(pl.multiple_of(pl.program_id(0) * step, step), step)
    if len(outs) > 2:
        outs[2][...] = dense[depth:, columns]
    for side in range(2):
        part = rows[side * height : (side + 1) * height]
        sums = jnp.dot(part, dense[:depth, columns], preferred_element_type=jnp.float32)
        outs[side][...] = sums.astype(outs[side].dtype)


def first_shares(chunks, positions, sources, tiles_each, size, dtype):
    owners, height, lanes = chunks[0].shape
    depth = len(chunks) * owners * lanes // 2
    step = largest_divisor(size, 256)
    whole = lambda j, s: (0, 0, 0)
    heights = [height] * 2 + ([size - depth] if depth < size else [])
    kinds = [dtype] * 2 + [sources[0].dtype]
    return pl.pallas_call(
        functools.partial(first_kernel, len(chunks), len(sources), tiles_each),
        grid_spec=pltpu.PrefetchScalarGridSpec(
            num_scalar_prefetch=1,
            grid=(size // step,),
            in_specs=[pl.BlockSpec(array.shape, whole) for array in [*chunks, *sources]],
            out_specs=[pl.BlockSpec((tall, step), lambda j, s: (0, j)) for tall in heights],
            scratch_shapes=[
                pltpu.VMEM((size, size), sources[0].dtype),
                pltpu.VMEM((2 * height, depth), jnp.bfloat16),
            ],
        ),
        out_shape=[jax.ShapeDtypeStruct((tall, size), kind) for tall, kind in zip(heights, kinds)],
        cost_estimate=SMALL,
        compiler_params=pltpu.CompilerParams(vmem_limit_bytes=VMEM_MOST),
        name="first_shares",
    )(positions, *chunks, *sources)


def last_kernel(chunk, metric, one, two, out, rows):
    height = chunk.shape[1]

    @pl.when(pl.program_id(0) == 0)
    def _():
        unpack_rows([chunk], rows)

    for side, before in enumerate((one, two)):
        part = rows[side * height : (side + 1) * height]
        sums = jnp.dot(part, metric[...], preferred_element_type=jnp.float32)
        out[side] = (sums + before[...]).astype(out.dtype)


def last_share(chunk, metric, one, two):
    owners, height, lanes = chunk.shape
    depth, size = metric.shape
    step = largest_divisor(size, 256)
    tall = pl.BlockSpec((height, step), lambda j: (0, j))
    return pl.pallas_call(
        last_kernel,
        grid=(size // step,),
        in_specs=[
            pl.BlockSpec(chunk.shape, lambda j: (0, 0, 0)),
            pl.BlockSpec((depth, step), lambda j: (0, j)),
            tall,
            tall,
        ],
        out_specs=pl.BlockSpec((2, height, step), lambda j: (0, 0, j)),
        out_shape=jax.ShapeDtypeStruct((2, height, size), jnp.bfloat16),
        scratch_shapes=[pltpu.VMEM((2 * height, depth), jnp.bfloat16)],
        cost_estimate=SMALL,
        compiler_params=pltpu.CompilerParams(vmem_limit_bytes=VMEM_PART),
        name="last_share",
    )(chunk, metric, one, two)


def after(value, others):
    return lax.optimization_barrier((value, others))[0]


def shards(orb_count, aux_count, factors, amplitudes, partners, metric_tiles, tile_pos):
    group, domain, part = factors.shape
    span = metric_tiles.shape[1]
    width = span // 2
    chunk_count = part // width
    far_count = orb_count // 2
    me = lax.axis_index("orb")

    def to_far(array, shift):
        moves = [(g, (g + 2 * shift) % orb_count) for g in range(orb_count)]
        return lax.ppermute(array, "orb", moves)

    def to_mate(array):
        return lax.ppermute(array, "orb", [(g, g ^ 1) for g in range(orb_count)])

    owner, place = partners // group, partners % group
    far = (me // 2 - owner // 2) % far_count
    slots = ((far * 2 + (me % 2 + owner) % 2) * group + place).reshape(-1)

    half_tiles = metric_tiles.shape[0] // 2
    mine = (me % 2) * half_tiles
    tiles = lax.dynamic_slice_in_dim(metric_tiles, mine, half_tiles, axis=0).reshape(half_tiles * span, span)
    spots = lax.dynamic_slice_in_dim(tile_pos, mine, half_tiles, axis=0).reshape(-1).astype(tiles.dtype)
    spot_rows = -(-spots.size // (16 * span)) * 16
    spots = jnp.pad(spots, (0, spot_rows * span - spots.size)).reshape(spot_rows, span)
    load = jnp.concatenate([tiles, spots], axis=0)
    parts = [load]
    for shift in range(1, aux_count // 2):
        moves = [(g, (g + 2 * shift) % aux_count) for g in range(aux_count)]
        parts.append(lax.ppermute(load, "aux", moves))

    packed = list(pack_chunks(factors, width, 0, 1))
    if chunk_count > 1:
        packed += pack_chunks(factors, width, 1, chunk_count - 1)
        parts = after(parts, packed[1:])

    column = join(parts)
    beside = lax.ppermute(column, "aux", [(g, g ^ 1) for g in range(aux_count)])
    sources = [column, beside, to_mate(column), to_mate(beside)]

    before_products = {1: column, 2: beside, 3: sources[2:]}
    products = []
    far_pieces, made = [], None
    for at in range(chunk_count):
        own = packed[at]
        if at:
            own = after(own, far_pieces)
        far_pieces = [to_far(own, shift) for shift in range(1, far_count)]
        if chunk_count > 1:
            far_pieces = after(far_pieces, made if at else [packed[1:], parts[1::2]])
        pieces = []
        for piece in [packed[at]] + far_pieces:
            pieces += [piece, to_mate(piece)]
        places = after(slots, before_products[at]) if at in before_products else slots
        made = chunk_products(places, amplitudes, pieces, aux_count)
        products.append(lax.all_to_all(made, "aux", split_axis=0, concat_axis=0, tiled=True))

    positions = jnp.concatenate([source[:, half_tiles * span, : 2 * half_tiles] for source in sources])
    positions = positions.astype(jnp.int32).reshape(-1)
    size = part * aux_count
    if chunk_count > 1:
        ready = after(products[:-1], made)
        one, two, metric = first_shares(ready, positions, sources, half_tiles, size, jnp.float32)
        result = last_share(products[-1], metric, one, two)
    else:
        result = jnp.stack(first_shares(products, positions, sources, half_tiles, size, jnp.bfloat16))
    return result.reshape(group, domain // aux_count, size)


def solution(mesh):
    in_specs = (
        P("orb", None, "aux"),
        P("orb", None, None, None),
        P("orb", None),
        P("aux", None, None),
        P("aux", None),
    )
    body = functools.partial(shards, mesh.shape["orb"], mesh.shape["aux"])
    return jax.shard_map(body, mesh=mesh, in_specs=in_specs, out_specs=P("orb", "aux", None), check_vma=False)
```

```python
import functools

import jax
import jax.numpy as jnp
from jax import lax
from jax.experimental import pallas as pl
from jax.experimental.pallas import tpu as pltpu
from jax.sharding import PartitionSpec as P

VMEM_WHOLE = 58 * 1024 * 1024
VMEM_MOST = 44 * 1024 * 1024
VMEM_PART = 44 * 1024 * 1024
SMALL = pl.CostEstimate(flops=0, bytes_accessed=4096, transcendentals=0)
LARGE = pl.CostEstimate(flops=40_000_000_000, bytes_accessed=4096, transcendentals=0)


def largest_divisor(total, most):
    return max(size for size in range(1, most + 1) if total % size == 0)


def pack_kernel(width, first, source, *chunks):
    half = source.shape[1] // 2
    for at, chunk in enumerate(chunks):
        columns = slice(first + at * width, first + (at + 1) * width)
        chunk[...] = jnp.concatenate([source[:, :half, columns], source[:, half:, columns]], axis=-1)


def pack_chunks(factors, width, begin, count):
    orbitals, domain, part = factors.shape
    first = begin * width
    step = largest_divisor(orbitals, 12)
    packed = (step, domain // 2, 2 * width)
    return pl.pallas_call(
        functools.partial(pack_kernel, width, first),
        grid=(orbitals // step,),
        in_specs=[pl.BlockSpec((step, domain, part), lambda i: (i, 0, 0))],
        out_specs=[pl.BlockSpec(packed, lambda i: (i, 0, 0))] * count,
        out_shape=[jax.ShapeDtypeStruct((orbitals,) + packed[1:], factors.dtype)] * count,
        cost_estimate=SMALL,
        compiler_params=pltpu.CompilerParams(vmem_limit_bytes=VMEM_WHOLE),
        name="pack_chunks",
    )(factors)


def halves_apart(one, two, half):
    lower = jnp.concatenate([one[:, :half], two[:, :half]], axis=1)
    upper = jnp.concatenate([one[:, half:], two[:, half:]], axis=1)
    return lower, upper


def product_kernel(pairs, split_rows, streams, slots, *refs):
    amplitudes, pieces = refs[: 2 * streams], refs[2 * streams : -3]
    out, table, arrived = refs[-3:]
    group, half_domain, lanes = pieces[0].shape
    here = pl.program_id(0)

    @pl.when(here == 0)
    def _():
        copies = [
            pltpu.make_async_copy(piece, table.at[pl.ds(at * group, group)], arrived.at[at])
            for at, piece in enumerate(pieces)
        ]
        for copy in copies:
            copy.start()
        for copy in copies:
            copy.wait()

    step, domain = amplitudes[0].shape[1], amplitudes[0].shape[3]
    each = pairs // streams
    half_count = pl.num_programs(0) * step
    first = lax.broadcasted_iota(jnp.int32, (domain, lanes), 1) < lanes // 2
    for q in range(step):
        sums = []
        for side in range(2):
            base = (side * half_count + here * step + q) * pairs
            lower, upper = [], []
            for k in range(0, pairs, 2):
                tiles = amplitudes[side * streams + k // each]
                low, high = halves_apart(tiles[0, q, k % each], tiles[0, q, k % each + 1], half_domain)
                lower.append(low)
                upper.append(high)
            left = jnp.concatenate([jnp.concatenate(lower, axis=1), jnp.concatenate(upper, axis=1)], axis=0)
            right = jnp.concatenate([table[slots[base + k]] for k in range(pairs)], axis=0)
            sums.append(jnp.dot(left, right, preferred_element_type=jnp.float32))
        placed = jnp.where(first, sums[0][:domain], sums[1][domain:])
        moved = jnp.where(first, sums[1][:domain], sums[0][domain:])
        both = (placed + pltpu.roll(moved, lanes // 2, 1)).astype(out.dtype)
        if split_rows:
            owners, rows = out.shape[0], domain // out.shape[0]
            out[:, q * rows : (q + 1) * rows, :] = both.reshape(owners, rows, lanes)
        else:
            out[q] = both


def chunk_products(slots, amplitudes, pieces, owners, cost):
    orbitals, pairs, domain, _ = amplitudes.shape
    group, half_domain, lanes = pieces[0].shape
    total = group * len(pieces)
    half = orbitals // 2
    rows = domain // owners
    split_rows = rows % 16 == 0
    step = largest_divisor(half, 4)
    streams = 2 if pairs % 4 == 0 else 1
    tiles = (1, step, pairs // streams, domain, domain)
    if split_rows:
        out_shape, out_block, out_at = (owners, half * rows, lanes), (owners, step * rows, lanes), lambda i, s: (0, i, 0)
    else:
        out_shape, out_block, out_at = (half, domain, lanes), (step, domain, lanes), lambda i, s: (i, 0, 0)
    result = pl.pallas_call(
        functools.partial(product_kernel, pairs, split_rows, streams),
        grid_spec=pltpu.PrefetchScalarGridSpec(
            num_scalar_prefetch=1,
            grid=(half // step,),
            in_specs=[
                pl.BlockSpec(tiles, lambda i, s, side=side, part=part: (side, i, part, 0, 0))
                for side in range(2)
                for part in range(streams)
            ]
            + [pl.BlockSpec(memory_space=pl.ANY)] * len(pieces),
            out_specs=pl.BlockSpec(out_block, out_at),
            scratch_shapes=[
                pltpu.VMEM((total, half_domain, lanes), jnp.bfloat16),
                pltpu.SemaphoreType.DMA((len(pieces),)),
            ],
        ),
        out_shape=jax.ShapeDtypeStruct(out_shape, jnp.bfloat16),
        cost_estimate=cost,
        compiler_params=pltpu.CompilerParams(vmem_limit_bytes=VMEM_PART),
        name="chunk_products",
    )(slots, *[amplitudes.reshape(2, half, pairs, domain, domain)] * (2 * streams), *pieces)
    if split_rows:
        return result
    result = result.reshape(half, owners, rows, lanes).transpose(1, 0, 2, 3)
    return result.reshape(owners, half * rows, lanes)


def join_kernel(*refs):
    for at, piece in enumerate(refs[:-1]):
        refs[-1][at] = piece[...]


def join(pieces):
    shape = (len(pieces),) + pieces[0].shape
    return pl.pallas_call(
        join_kernel,
        out_shape=jax.ShapeDtypeStruct(shape, pieces[0].dtype),
        cost_estimate=SMALL,
        compiler_params=pltpu.CompilerParams(vmem_limit_bytes=VMEM_PART),
        name="join",
    )(*pieces)


def place_tiles(chunks, owners, tiles_each, positions, sources, dense):
    devices, _, span = sources[0].shape
    width = span // 2
    dense[...] = jnp.zeros_like(dense)
    for which, source in enumerate(sources):

        @pl.loop(0, devices)
        def _(device):
            for at in range(tiles_each):
                number = (which * devices + device) * tiles_each + at
                column = pl.multiple_of(positions[2 * number + 1] * span, span)
                for side in range(2):
                    block = 2 * positions[2 * number] + side
                    row = ((block % chunks) * owners + block // chunks) * width
                    begin = at * span + side * width
                    dense[pl.ds(pl.multiple_of(row, width), width), pl.ds(column, span)] = source[
                        device, begin : begin + width, :
                    ]


def unpack_rows(chunks, rows):
    owners, height, lanes = chunks[0].shape
    width = lanes // 2
    for at, chunk in enumerate(chunks):
        for owner in range(0, owners, 2):
            one, two = chunk[owner], chunk[owner + 1]
            columns = pl.ds((at * owners + owner) * width, lanes)
            rows[:height, columns] = jnp.concatenate([one[:, :width], two[:, :width]], axis=1)
            rows[height:, columns] = jnp.concatenate([one[:, width:], two[:, width:]], axis=1)


def first_kernel(count, source_count, tiles_each, positions, *refs):
    chunks, sources = refs[:count], refs[count : count + source_count]
    *outs, dense, rows = refs[count + source_count :]
    owners, height, _ = chunks[0].shape
    depth = rows.shape[1]

    @pl.when(pl.program_id(0) == 0)
    def _():
        place_tiles(dense.shape[0] // (depth // count), owners, tiles_each, positions, sources, dense)
        unpack_rows(chunks, rows)

    step = outs[0].shape[-1]
    columns = pl.ds(pl.multiple_of(pl.program_id(0) * step, step), step)
    if len(outs) > 2:
        outs[2][...] = dense[depth:, columns]
    for side in range(2):
        part = rows[side * height : (side + 1) * height]
        sums = jnp.dot(part, dense[:depth, columns], preferred_element_type=jnp.float32)
        outs[side][...] = sums.astype(outs[side].dtype)


def first_shares(chunks, positions, sources, tiles_each, size, dtype):
    owners, height, lanes = chunks[0].shape
    depth = len(chunks) * owners * lanes // 2
    step = largest_divisor(size, 256)
    whole = lambda j, s: (0, 0, 0)
    heights = [height] * 2 + ([size - depth] if depth < size else [])
    kinds = [dtype] * 2 + [sources[0].dtype]
    return pl.pallas_call(
        functools.partial(first_kernel, len(chunks), len(sources), tiles_each),
        grid_spec=pltpu.PrefetchScalarGridSpec(
            num_scalar_prefetch=1,
            grid=(size // step,),
            in_specs=[pl.BlockSpec(array.shape, whole) for array in [*chunks, *sources]],
            out_specs=[pl.BlockSpec((tall, step), lambda j, s: (0, j)) for tall in heights],
            scratch_shapes=[
                pltpu.VMEM((size, size), sources[0].dtype),
                pltpu.VMEM((2 * height, depth), jnp.bfloat16),
            ],
        ),
        out_shape=[jax.ShapeDtypeStruct((tall, size), kind) for tall, kind in zip(heights, kinds)],
        cost_estimate=SMALL,
        compiler_params=pltpu.CompilerParams(vmem_limit_bytes=VMEM_MOST),
        name="first_shares",
    )(positions, *chunks, *sources)


def last_kernel(chunk, metric, one, two, out, rows):
    height = chunk.shape[1]

    @pl.when(pl.program_id(0) == 0)
    def _():
        unpack_rows([chunk], rows)

    for side, before in enumerate((one, two)):
        part = rows[side * height : (side + 1) * height]
        sums = jnp.dot(part, metric[...], preferred_element_type=jnp.float32)
        out[side] = (sums + before[...]).astype(out.dtype)


def last_share(chunk, metric, one, two):
    owners, height, lanes = chunk.shape
    depth, size = metric.shape
    step = largest_divisor(size, 256)
    tall = pl.BlockSpec((height, step), lambda j: (0, j))
    return pl.pallas_call(
        last_kernel,
        grid=(size // step,),
        in_specs=[
            pl.BlockSpec(chunk.shape, lambda j: (0, 0, 0)),
            pl.BlockSpec((depth, step), lambda j: (0, j)),
            tall,
            tall,
        ],
        out_specs=pl.BlockSpec((2, height, step), lambda j: (0, 0, j)),
        out_shape=jax.ShapeDtypeStruct((2, height, size), jnp.bfloat16),
        scratch_shapes=[pltpu.VMEM((2 * height, depth), jnp.bfloat16)],
        cost_estimate=SMALL,
        compiler_params=pltpu.CompilerParams(vmem_limit_bytes=VMEM_PART),
        name="last_share",
    )(chunk, metric, one, two)


def after(value, others):
    return lax.optimization_barrier((value, others))[0]


def shards(orb_count, aux_count, factors, amplitudes, partners, metric_tiles, tile_pos):
    group, domain, part = factors.shape
    span = metric_tiles.shape[1]
    width = span // 2
    chunk_count = part // width
    far_count = orb_count // 2
    me = lax.axis_index("orb")

    def to_far(array, shift):
        moves = [(g, (g + 2 * shift) % orb_count) for g in range(orb_count)]
        return lax.ppermute(array, "orb", moves)

    def to_mate(array):
        return lax.ppermute(array, "orb", [(g, g ^ 1) for g in range(orb_count)])

    owner, place = partners // group, partners % group
    far = (me // 2 - owner // 2) % far_count
    slots = ((far * 2 + (me % 2 + owner) % 2) * group + place).reshape(-1)

    half_tiles = metric_tiles.shape[0] // 2
    mine = (me % 2) * half_tiles
    tiles = lax.dynamic_slice_in_dim(metric_tiles, mine, half_tiles, axis=0).reshape(half_tiles * span, span)
    spots = lax.dynamic_slice_in_dim(tile_pos, mine, half_tiles, axis=0).reshape(-1).astype(tiles.dtype)
    spot_rows = -(-spots.size // (16 * span)) * 16
    spots = jnp.pad(spots, (0, spot_rows * span - spots.size)).reshape(spot_rows, span)
    load = jnp.concatenate([tiles, spots], axis=0)
    parts = [load]
    for shift in range(1, aux_count // 2):
        moves = [(g, (g + 2 * shift) % aux_count) for g in range(aux_count)]
        parts.append(lax.ppermute(load, "aux", moves))

    packed = list(pack_chunks(factors, width, 0, 1))
    if chunk_count > 1:
        packed += pack_chunks(factors, width, 1, chunk_count - 1)
        parts = [after(part, packed[1:]) for part in parts]

    column = join(parts)
    beside = lax.ppermute(column, "aux", [(g, g ^ 1) for g in range(aux_count)])
    sources = [column, beside, to_mate(column), to_mate(beside)]

    before_products = {1: column, 2: beside, 3: sources[2:]}
    products = []
    far_pieces, made = [], None
    for at in range(chunk_count):
        own = packed[at]
        if at:
            own = after(own, far_pieces)
        far_pieces = [to_far(own, shift) for shift in range(1, far_count)]
        if chunk_count > 1:
            far_pieces = after(far_pieces, made if at else [packed[1:], parts[1::2]])
        pieces = []
        for piece in [packed[at]] + far_pieces:
            pieces += [piece, to_mate(piece)]
        places = after(slots, before_products[at]) if at in before_products else slots
        made = chunk_products(places, amplitudes, pieces, aux_count, LARGE if at < 2 else SMALL)
        products.append(lax.all_to_all(made, "aux", split_axis=0, concat_axis=0, tiled=True))

    positions = jnp.concatenate([source[:, half_tiles * span, : 2 * half_tiles] for source in sources])
    positions = positions.astype(jnp.int32).reshape(-1)
    size = part * aux_count
    if chunk_count > 1:
        ready = after(products[:-1], made)
        one, two, metric = first_shares(ready, positions, sources, half_tiles, size, jnp.float32)
        result = last_share(products[-1], metric, one, two)
    else:
        result = jnp.stack(first_shares(products, positions, sources, half_tiles, size, jnp.bfloat16))
    return result.reshape(group, domain // aux_count, size)


def solution(mesh):
    in_specs = (
        P("orb", None, "aux"),
        P("orb", None, None, None),
        P("orb", None),
        P("aux", None, None),
        P("aux", None),
    )
    body = functools.partial(shards, mesh.shape["orb"], mesh.shape["aux"])
    return jax.shard_map(body, mesh=mesh, in_specs=in_specs, out_specs=P("orb", "aux", None), check_vma=False)
```

```python
import functools

import jax
import jax.numpy as jnp
from jax import lax
from jax.experimental import pallas as pl
from jax.experimental.pallas import tpu as pltpu
from jax.sharding import PartitionSpec as P

VMEM_WHOLE = 58 * 1024 * 1024
VMEM_MOST = 44 * 1024 * 1024
VMEM_PART = 44 * 1024 * 1024
SMALL = pl.CostEstimate(flops=0, bytes_accessed=4096, transcendentals=0)


def largest_divisor(total, most):
    return max(size for size in range(1, most + 1) if total % size == 0)


def pack_kernel(width, first, source, *chunks):
    half = source.shape[1] // 2
    for at, chunk in enumerate(chunks):
        columns = slice(first + at * width, first + (at + 1) * width)
        chunk[...] = jnp.concatenate([source[:, :half, columns], source[:, half:, columns]], axis=-1)


def pack_chunks(factors, width, begin, count):
    orbitals, domain, part = factors.shape
    first = begin * width
    step = largest_divisor(orbitals, 12)
    packed = (step, domain // 2, 2 * width)
    return pl.pallas_call(
        functools.partial(pack_kernel, width, first),
        grid=(orbitals // step,),
        in_specs=[pl.BlockSpec((step, domain, part), lambda i: (i, 0, 0))],
        out_specs=[pl.BlockSpec(packed, lambda i: (i, 0, 0))] * count,
        out_shape=[jax.ShapeDtypeStruct((orbitals,) + packed[1:], factors.dtype)] * count,
        cost_estimate=SMALL,
        compiler_params=pltpu.CompilerParams(vmem_limit_bytes=VMEM_WHOLE),
        name="pack_chunks",
    )(factors)


def halves_apart(one, two, half):
    lower = jnp.concatenate([one[:, :half], two[:, :half]], axis=1)
    upper = jnp.concatenate([one[:, half:], two[:, half:]], axis=1)
    return lower, upper


def product_kernel(pairs, split_rows, streams, slots, *refs):
    amplitudes, pieces = refs[: 2 * streams], refs[2 * streams : -3]
    out, table, arrived = refs[-3:]
    group, half_domain, lanes = pieces[0].shape
    here = pl.program_id(0)

    @pl.when(here == 0)
    def _():
        copies = [
            pltpu.make_async_copy(piece, table.at[pl.ds(at * group, group)], arrived.at[at])
            for at, piece in enumerate(pieces)
        ]
        for copy in copies:
            copy.start()
        for copy in copies:
            copy.wait()

    step, domain = amplitudes[0].shape[1], amplitudes[0].shape[3]
    each = pairs // streams
    half_count = pl.num_programs(0) * step
    first = lax.broadcasted_iota(jnp.int32, (domain, lanes), 1) < lanes // 2
    for q in range(step):
        sums = []
        for side in range(2):
            base = (side * half_count + here * step + q) * pairs
            lower, upper = [], []
            for k in range(0, pairs, 2):
                tiles = amplitudes[side * streams + k // each]
                low, high = halves_apart(tiles[0, q, k % each], tiles[0, q, k % each + 1], half_domain)
                lower.append(low)
                upper.append(high)
            left = jnp.concatenate([jnp.concatenate(lower, axis=1), jnp.concatenate(upper, axis=1)], axis=0)
            right = jnp.concatenate([table[slots[base + k]] for k in range(pairs)], axis=0)
            sums.append(jnp.dot(left, right, preferred_element_type=jnp.float32))
        placed = jnp.where(first, sums[0][:domain], sums[1][domain:])
        moved = jnp.where(first, sums[1][:domain], sums[0][domain:])
        both = (placed + pltpu.roll(moved, lanes // 2, 1)).astype(out.dtype)
        if split_rows:
            owners, rows = out.shape[0], domain // out.shape[0]
            out[:, q * rows : (q + 1) * rows, :] = both.reshape(owners, rows, lanes)
        else:
            out[q] = both


def chunk_products(slots, amplitudes, pieces, owners):
    orbitals, pairs, domain, _ = amplitudes.shape
    group, half_domain, lanes = pieces[0].shape
    total = group * len(pieces)
    half = orbitals // 2
    rows = domain // owners
    split_rows = rows % 16 == 0
    step = largest_divisor(half, 4)
    streams = 2 if pairs % 4 == 0 else 1
    tiles = (1, step, pairs // streams, domain, domain)
    if split_rows:
        out_shape, out_block, out_at = (owners, half * rows, lanes), (owners, step * rows, lanes), lambda i, s: (0, i, 0)
    else:
        out_shape, out_block, out_at = (half, domain, lanes), (step, domain, lanes), lambda i, s: (i, 0, 0)
    result = pl.pallas_call(
        functools.partial(product_kernel, pairs, split_rows, streams),
        grid_spec=pltpu.PrefetchScalarGridSpec(
            num_scalar_prefetch=1,
            grid=(half // step,),
            in_specs=[
                pl.BlockSpec(tiles, lambda i, s, side=side, part=part: (side, i, part, 0, 0))
                for side in range(2)
                for part in range(streams)
            ]
            + [pl.BlockSpec(memory_space=pl.ANY)] * len(pieces),
            out_specs=pl.BlockSpec(out_block, out_at),
            scratch_shapes=[
                pltpu.VMEM((total, half_domain, lanes), jnp.bfloat16),
                pltpu.SemaphoreType.DMA((len(pieces),)),
            ],
        ),
        out_shape=jax.ShapeDtypeStruct(out_shape, jnp.bfloat16),
        cost_estimate=SMALL,
        compiler_params=pltpu.CompilerParams(vmem_limit_bytes=VMEM_PART),
        name="chunk_products",
    )(slots, *[amplitudes.reshape(2, half, pairs, domain, domain)] * (2 * streams), *pieces)
    if split_rows:
        return result
    result = result.reshape(half, owners, rows, lanes).transpose(1, 0, 2, 3)
    return result.reshape(owners, half * rows, lanes)


def place_tiles(chunks, owners, tiles_each, positions, sources, dense):
    devices, _, span = sources[0].shape
    width = span // 2
    dense[...] = jnp.zeros_like(dense)
    for which, source in enumerate(sources):

        @pl.loop(0, devices)
        def _(device):
            for at in range(tiles_each):
                number = (which * devices + device) * tiles_each + at
                column = pl.multiple_of(positions[2 * number + 1] * span, span)
                for side in range(2):
                    block = 2 * positions[2 * number] + side
                    row = ((block % chunks) * owners + block // chunks) * width
                    begin = at * span + side * width
                    dense[pl.ds(pl.multiple_of(row, width), width), pl.ds(column, span)] = source[
                        device, begin : begin + width, :
                    ]


def unpack_rows(chunks, rows):
    owners, height, lanes = chunks[0].shape
    width = lanes // 2
    for at, chunk in enumerate(chunks):
        for owner in range(0, owners, 2):
            one, two = chunk[owner], chunk[owner + 1]
            columns = pl.ds((at * owners + owner) * width, lanes)
            rows[:height, columns] = jnp.concatenate([one[:, :width], two[:, :width]], axis=1)
            rows[height:, columns] = jnp.concatenate([one[:, width:], two[:, width:]], axis=1)


def first_kernel(count, source_count, tiles_each, positions, *refs):
    chunks, sources = refs[:count], refs[count : count + source_count]
    *outs, dense, rows = refs[count + source_count :]
    owners, height, _ = chunks[0].shape
    depth = rows.shape[1]

    @pl.when(pl.program_id(0) == 0)
    def _():
        place_tiles(dense.shape[0] // (depth // count), owners, tiles_each, positions, sources, dense)
        unpack_rows(chunks, rows)

    step = outs[0].shape[-1]
    columns = pl.ds(pl.multiple_of(pl.program_id(0) * step, step), step)
    if len(outs) > 2:
        outs[2][...] = dense[depth:, columns]
    for side in range(2):
        part = rows[side * height : (side + 1) * height]
        sums = jnp.dot(part, dense[:depth, columns], preferred_element_type=jnp.float32)
        outs[side][...] = sums.astype(outs[side].dtype)


def first_shares(chunks, positions, sources, tiles_each, size, dtype):
    owners, height, lanes = chunks[0].shape
    depth = len(chunks) * owners * lanes // 2
    step = largest_divisor(size, 256)
    whole = lambda j, s: (0, 0, 0)
    heights = [height] * 2 + ([size - depth] if depth < size else [])
    kinds = [dtype] * 2 + [sources[0].dtype]
    return pl.pallas_call(
        functools.partial(first_kernel, len(chunks), len(sources), tiles_each),
        grid_spec=pltpu.PrefetchScalarGridSpec(
            num_scalar_prefetch=1,
            grid=(size // step,),
            in_specs=[pl.BlockSpec(array.shape, whole) for array in [*chunks, *sources]],
            out_specs=[pl.BlockSpec((tall, step), lambda j, s: (0, j)) for tall in heights],
            scratch_shapes=[
                pltpu.VMEM((size, size), sources[0].dtype),
                pltpu.VMEM((2 * height, depth), jnp.bfloat16),
            ],
        ),
        out_shape=[jax.ShapeDtypeStruct((tall, size), kind) for tall, kind in zip(heights, kinds)],
        cost_estimate=SMALL,
        compiler_params=pltpu.CompilerParams(vmem_limit_bytes=VMEM_MOST),
        name="first_shares",
    )(positions, *chunks, *sources)


def last_kernel(chunk, metric, one, two, out, rows):
    height = chunk.shape[1]

    @pl.when(pl.program_id(0) == 0)
    def _():
        unpack_rows([chunk], rows)

    for side, before in enumerate((one, two)):
        part = rows[side * height : (side + 1) * height]
        sums = jnp.dot(part, metric[...], preferred_element_type=jnp.float32)
        out[side] = (sums + before[...]).astype(out.dtype)


def last_share(chunk, metric, one, two):
    owners, height, lanes = chunk.shape
    depth, size = metric.shape
    step = largest_divisor(size, 256)
    tall = pl.BlockSpec((height, step), lambda j: (0, j))
    return pl.pallas_call(
        last_kernel,
        grid=(size // step,),
        in_specs=[
            pl.BlockSpec(chunk.shape, lambda j: (0, 0, 0)),
            pl.BlockSpec((depth, step), lambda j: (0, j)),
            tall,
            tall,
        ],
        out_specs=pl.BlockSpec((2, height, step), lambda j: (0, 0, j)),
        out_shape=jax.ShapeDtypeStruct((2, height, size), jnp.bfloat16),
        scratch_shapes=[pltpu.VMEM((2 * height, depth), jnp.bfloat16)],
        cost_estimate=SMALL,
        compiler_params=pltpu.CompilerParams(vmem_limit_bytes=VMEM_PART),
        name="last_share",
    )(chunk, metric, one, two)


def after(value, others):
    return lax.optimization_barrier((value, others))[0]


def shards(orb_count, aux_count, factors, amplitudes, partners, metric_tiles, tile_pos):
    group, domain, part = factors.shape
    span = metric_tiles.shape[1]
    width = span // 2
    chunk_count = part // width
    far_count = orb_count // 2
    me = lax.axis_index("orb")

    def to_far(array, shift):
        moves = [(g, (g + 2 * shift) % orb_count) for g in range(orb_count)]
        return lax.ppermute(array, "orb", moves)

    def to_mate(array):
        return lax.ppermute(array, "orb", [(g, g ^ 1) for g in range(orb_count)])

    owner, place = partners // group, partners % group
    far = (me // 2 - owner // 2) % far_count
    slots = ((far * 2 + (me % 2 + owner) % 2) * group + place).reshape(-1)

    half_tiles = metric_tiles.shape[0] // 2
    mine = (me % 2) * half_tiles
    tiles = lax.dynamic_slice_in_dim(metric_tiles, mine, half_tiles, axis=0).reshape(half_tiles * span, span)
    spots = lax.dynamic_slice_in_dim(tile_pos, mine, half_tiles, axis=0).reshape(-1).astype(tiles.dtype)
    spot_rows = -(-spots.size // (16 * span)) * 16
    spots = jnp.pad(spots, (0, spot_rows * span - spots.size)).reshape(spot_rows, span)
    load = jnp.concatenate([tiles, spots], axis=0)
    first = lax.all_gather(load[None], "aux", axis=0, tiled=True)
    sources = [first, to_mate(first)]

    packed = list(pack_chunks(factors, width, 0, 1))
    if chunk_count > 1:
        packed += pack_chunks(factors, width, 1, chunk_count - 1)

    before_products = {3: sources}
    products = []
    far_pieces, made = [], None
    for at in range(chunk_count):
        own = packed[at]
        if at:
            own = after(own, far_pieces)
        far_pieces = [to_far(own, shift) for shift in range(1, far_count)]
        if chunk_count > 1:
            far_pieces = after(far_pieces, made if at else packed[1:])
        pieces = []
        for piece in [packed[at]] + far_pieces:
            pieces += [piece, to_mate(piece)]
        places = after(slots, before_products[at]) if at in before_products else slots
        made = chunk_products(places, amplitudes, pieces, aux_count)
        products.append(lax.all_to_all(made, "aux", split_axis=0, concat_axis=0, tiled=True))

    positions = jnp.concatenate([source[:, half_tiles * span, : 2 * half_tiles] for source in sources])
    positions = positions.astype(jnp.int32).reshape(-1)
    size = part * aux_count
    if chunk_count > 1:
        ready = after(products[:-1], made)
        one, two, metric = first_shares(ready, positions, sources, half_tiles, size, jnp.float32)
        result = last_share(products[-1], metric, one, two)
    else:
        result = jnp.stack(first_shares(products, positions, sources, half_tiles, size, jnp.bfloat16))
    return result.reshape(group, domain // aux_count, size)


def solution(mesh):
    in_specs = (
        P("orb", None, "aux"),
        P("orb", None, None, None),
        P("orb", None),
        P("aux", None, None),
        P("aux", None),
    )
    body = functools.partial(shards, mesh.shape["orb"], mesh.shape["aux"])
    return jax.shard_map(body, mesh=mesh, in_specs=in_specs, out_specs=P("orb", "aux", None), check_vma=False)
```

```python
import functools

import jax
import jax.numpy as jnp
from jax import lax
from jax.experimental import pallas as pl
from jax.experimental.pallas import tpu as pltpu
from jax.sharding import PartitionSpec as P

VMEM_WHOLE = 58 * 1024 * 1024
VMEM_MOST = 30 * 1024 * 1024
VMEM_LAST = 16 * 1024 * 1024
VMEM_PART = 44 * 1024 * 1024
SMALL = pl.CostEstimate(flops=0, bytes_accessed=4096, transcendentals=0)


def largest_divisor(total, most):
    return max(size for size in range(1, most + 1) if total % size == 0)


def pack_kernel(width, first, source, *chunks):
    half = source.shape[1] // 2
    for at, chunk in enumerate(chunks):
        columns = slice(first + at * width, first + (at + 1) * width)
        chunk[...] = jnp.concatenate([source[:, :half, columns], source[:, half:, columns]], axis=-1)


def pack_chunks(factors, width, begin, count):
    orbitals, domain, part = factors.shape
    first = begin * width
    step = largest_divisor(orbitals, 12)
    packed = (step, domain // 2, 2 * width)
    return pl.pallas_call(
        functools.partial(pack_kernel, width, first),
        grid=(orbitals // step,),
        in_specs=[pl.BlockSpec((step, domain, part), lambda i: (i, 0, 0))],
        out_specs=[pl.BlockSpec(packed, lambda i: (i, 0, 0))] * count,
        out_shape=[jax.ShapeDtypeStruct((orbitals,) + packed[1:], factors.dtype)] * count,
        cost_estimate=SMALL,
        compiler_params=pltpu.CompilerParams(vmem_limit_bytes=VMEM_WHOLE),
        name="pack_chunks",
    )(factors)


def halves_apart(one, two, half):
    lower = jnp.concatenate([one[:, :half], two[:, :half]], axis=1)
    upper = jnp.concatenate([one[:, half:], two[:, half:]], axis=1)
    return lower, upper


def product_kernel(pairs, split_rows, streams, slots, *refs):
    amplitudes, pieces = refs[: 2 * streams], refs[2 * streams : -3]
    out, table, arrived = refs[-3:]
    group, half_domain, lanes = pieces[0].shape
    here = pl.program_id(0)

    @pl.when(here == 0)
    def _():
        copies = [
            pltpu.make_async_copy(piece, table.at[pl.ds(at * group, group)], arrived.at[at])
            for at, piece in enumerate(pieces)
        ]
        for copy in copies:
            copy.start()
        for copy in copies:
            copy.wait()

    step, domain = amplitudes[0].shape[1], amplitudes[0].shape[3]
    each = pairs // streams
    half_count = pl.num_programs(0) * step
    first = lax.broadcasted_iota(jnp.int32, (domain, lanes), 1) < lanes // 2
    for q in range(step):
        sums = []
        for side in range(2):
            base = (side * half_count + here * step + q) * pairs
            lower, upper = [], []
            for k in range(0, pairs, 2):
                tiles = amplitudes[side * streams + k // each]
                low, high = halves_apart(tiles[0, q, k % each], tiles[0, q, k % each + 1], half_domain)
                lower.append(low)
                upper.append(high)
            left = jnp.concatenate([jnp.concatenate(lower, axis=1), jnp.concatenate(upper, axis=1)], axis=0)
            right = jnp.concatenate([table[slots[base + k]] for k in range(pairs)], axis=0)
            sums.append(jnp.dot(left, right, preferred_element_type=jnp.float32))
        placed = jnp.where(first, sums[0][:domain], sums[1][domain:])
        moved = jnp.where(first, sums[1][:domain], sums[0][domain:])
        both = (placed + pltpu.roll(moved, lanes // 2, 1)).astype(out.dtype)
        if split_rows:
            owners, rows = out.shape[0], domain // out.shape[0]
            out[:, q * rows : (q + 1) * rows, :] = both.reshape(owners, rows, lanes)
        else:
            out[q] = both


def chunk_products(slots, amplitudes, pieces, owners):
    orbitals, pairs, domain, _ = amplitudes.shape
    group, half_domain, lanes = pieces[0].shape
    total = group * len(pieces)
    half = orbitals // 2
    rows = domain // owners
    split_rows = rows % 16 == 0
    step = largest_divisor(half, 4)
    streams = 2 if pairs % 4 == 0 else 1
    tiles = (1, step, pairs // streams, domain, domain)
    if split_rows:
        out_shape, out_block, out_at = (owners, half * rows, lanes), (owners, step * rows, lanes), lambda i, s: (0, i, 0)
    else:
        out_shape, out_block, out_at = (half, domain, lanes), (step, domain, lanes), lambda i, s: (i, 0, 0)
    result = pl.pallas_call(
        functools.partial(product_kernel, pairs, split_rows, streams),
        grid_spec=pltpu.PrefetchScalarGridSpec(
            num_scalar_prefetch=1,
            grid=(half // step,),
            in_specs=[
                pl.BlockSpec(tiles, lambda i, s, side=side, part=part: (side, i, part, 0, 0))
                for side in range(2)
                for part in range(streams)
            ]
            + [pl.BlockSpec(memory_space=pl.ANY)] * len(pieces),
            out_specs=pl.BlockSpec(out_block, out_at),
            scratch_shapes=[
                pltpu.VMEM((total, half_domain, lanes), jnp.bfloat16),
                pltpu.SemaphoreType.DMA((len(pieces),)),
            ],
        ),
        out_shape=jax.ShapeDtypeStruct(out_shape, jnp.bfloat16),
        cost_estimate=SMALL,
        compiler_params=pltpu.CompilerParams(vmem_limit_bytes=VMEM_PART),
        name="chunk_products",
    )(slots, *[amplitudes.reshape(2, half, pairs, domain, domain)] * (2 * streams), *pieces)
    if split_rows:
        return result
    result = result.reshape(half, owners, rows, lanes).transpose(1, 0, 2, 3)
    return result.reshape(owners, half * rows, lanes)


def place_tiles(chunks, owners, tiles_each, positions, sources, dense):
    devices, _, span = sources[0].shape
    width = span // 2
    dense[...] = jnp.zeros_like(dense)
    for which, source in enumerate(sources):

        @pl.loop(0, devices)
        def _(device):
            for at in range(tiles_each):
                number = (which * devices + device) * tiles_each + at
                column = pl.multiple_of(positions[2 * number + 1] * span, span)
                for side in range(2):
                    block = 2 * positions[2 * number] + side
                    row = ((block % chunks) * owners + block // chunks) * width
                    begin = at * span + side * width
                    dense[pl.ds(pl.multiple_of(row, width), width), pl.ds(column, span)] = source[
                        device, begin : begin + width, :
                    ]


def unpack_rows(chunks, rows):
    owners, height, lanes = chunks[0].shape
    width = lanes // 2
    for at, chunk in enumerate(chunks):
        for owner in range(0, owners, 2):
            one, two = chunk[owner], chunk[owner + 1]
            columns = pl.ds((at * owners + owner) * width, lanes)
            rows[:height, columns] = jnp.concatenate([one[:, :width], two[:, :width]], axis=1)
            rows[height:, columns] = jnp.concatenate([one[:, width:], two[:, width:]], axis=1)


def first_kernel(count, source_count, tiles_each, positions, *refs):
    chunks, sources = refs[:count], refs[count : count + source_count]
    *outs, dense, rows = refs[count + source_count :]
    owners, height, _ = chunks[0].shape
    depth = rows.shape[1]

    @pl.when(pl.program_id(0) == 0)
    def _():
        place_tiles(dense.shape[0] // (depth // count), owners, tiles_each, positions, sources, dense)
        unpack_rows(chunks, rows)

    step = dense.shape[1] // pl.num_programs(0)
    columns = pl.ds(pl.multiple_of(pl.program_id(0) * step, step), step)
    if len(outs) > 1:
        outs[1][:, columns] = dense[depth:, columns]
    sums = jnp.dot(rows[...], dense[:depth, columns], preferred_element_type=jnp.float32)
    outs[0][:, columns] = sums.astype(outs[0].dtype)


def first_shares(chunks, positions, sources, tiles_each, size, dtype):
    owners, height, lanes = chunks[0].shape
    depth = len(chunks) * owners * lanes // 2
    step = largest_divisor(size, 256)
    whole = lambda j, s: (0, 0, 0)
    heights = [2 * height] + ([size - depth] if depth < size else [])
    kinds = [dtype, sources[0].dtype]
    return pl.pallas_call(
        functools.partial(first_kernel, len(chunks), len(sources), tiles_each),
        grid_spec=pltpu.PrefetchScalarGridSpec(
            num_scalar_prefetch=1,
            grid=(size // step,),
            in_specs=[pl.BlockSpec(array.shape, whole) for array in [*chunks, *sources]],
            out_specs=[pl.BlockSpec(memory_space=pltpu.VMEM)] * len(heights),
            scratch_shapes=[
                pltpu.VMEM((size, size), sources[0].dtype),
                pltpu.VMEM((2 * height, depth), jnp.bfloat16),
            ],
        ),
        out_shape=[pltpu.VMEM((tall, size), kind) for tall, kind in zip(heights, kinds)],
        cost_estimate=SMALL,
        compiler_params=pltpu.CompilerParams(vmem_limit_bytes=VMEM_MOST),
        name="first_shares",
    )(positions, *chunks, *sources)


def last_kernel(chunk, metric, before, out, rows):
    height = chunk.shape[1]

    @pl.when(pl.program_id(0) == 0)
    def _():
        unpack_rows([chunk], rows)

    step = out.shape[-1]
    columns = pl.ds(pl.multiple_of(pl.program_id(0) * step, step), step)
    sums = jnp.dot(rows[...], metric[:, columns], preferred_element_type=jnp.float32) + before[:, columns]
    out[0] = sums[:height].astype(out.dtype)
    out[1] = sums[height:].astype(out.dtype)


def last_share(chunk, metric, before):
    owners, height, lanes = chunk.shape
    depth, size = metric.shape
    step = largest_divisor(size, 256)
    return pl.pallas_call(
        last_kernel,
        grid=(size // step,),
        in_specs=[
            pl.BlockSpec(chunk.shape, lambda j: (0, 0, 0)),
            pl.BlockSpec(memory_space=pltpu.VMEM),
            pl.BlockSpec(memory_space=pltpu.VMEM),
        ],
        out_specs=pl.BlockSpec((2, height, step), lambda j: (0, 0, j)),
        out_shape=jax.ShapeDtypeStruct((2, height, size), jnp.bfloat16),
        scratch_shapes=[pltpu.VMEM((2 * height, depth), jnp.bfloat16)],
        cost_estimate=SMALL,
        compiler_params=pltpu.CompilerParams(vmem_limit_bytes=VMEM_LAST),
        name="last_share",
    )(chunk, metric, before)


def after(value, others):
    return lax.optimization_barrier((value, others))[0]


def shards(orb_count, aux_count, factors, amplitudes, partners, metric_tiles, tile_pos):
    group, domain, part = factors.shape
    span = metric_tiles.shape[1]
    width = span // 2
    chunk_count = part // width
    far_count = orb_count // 2
    me = lax.axis_index("orb")

    def to_far(array, shift):
        moves = [(g, (g + 2 * shift) % orb_count) for g in range(orb_count)]
        return lax.ppermute(array, "orb", moves)

    def to_mate(array):
        return lax.ppermute(array, "orb", [(g, g ^ 1) for g in range(orb_count)])

    owner, place = partners // group, partners % group
    far = (me // 2 - owner // 2) % far_count
    slots = ((far * 2 + (me % 2 + owner) % 2) * group + place).reshape(-1)

    half_tiles = metric_tiles.shape[0] // 2
    mine = (me % 2) * half_tiles
    tiles = lax.dynamic_slice_in_dim(metric_tiles, mine, half_tiles, axis=0).reshape(half_tiles * span, span)
    spots = lax.dynamic_slice_in_dim(tile_pos, mine, half_tiles, axis=0).reshape(-1).astype(tiles.dtype)
    spot_rows = -(-spots.size // (16 * span)) * 16
    spots = jnp.pad(spots, (0, spot_rows * span - spots.size)).reshape(spot_rows, span)
    load = jnp.concatenate([tiles, spots], axis=0)
    first = lax.all_gather(load[None], "aux", axis=0, tiled=True)
    sources = [first, to_mate(first)]

    packed = list(pack_chunks(factors, width, 0, 1))
    if chunk_count > 1:
        packed += pack_chunks(factors, width, 1, chunk_count - 1)

    before_products = {3: sources}
    products = []
    far_pieces, made = [], None
    for at in range(chunk_count):
        own = packed[at]
        if at:
            own = after(own, far_pieces)
        far_pieces = [to_far(own, shift) for shift in range(1, far_count)]
        if chunk_count > 1:
            far_pieces = after(far_pieces, made if at else packed[1:])
        pieces = []
        for piece in [packed[at]] + far_pieces:
            pieces += [piece, to_mate(piece)]
        places = after(slots, before_products[at]) if at in before_products else slots
        made = chunk_products(places, amplitudes, pieces, aux_count)
        products.append(lax.all_to_all(made, "aux", split_axis=0, concat_axis=0, tiled=True))

    positions = jnp.concatenate([source[:, half_tiles * span, : 2 * half_tiles] for source in sources])
    positions = positions.astype(jnp.int32).reshape(-1)
    size = part * aux_count
    if chunk_count > 1:
        ready = after(products[:-1], made)
        before, metric = first_shares(ready, positions, sources, half_tiles, size, jnp.float32)
        result = last_share(products[-1], metric, before)
    else:
        result = first_shares(products, positions, sources, half_tiles, size, jnp.bfloat16)[0]
        result = result.reshape(2, group // 2, domain // aux_count, size)
    return result.reshape(group, domain // aux_count, size)


def solution(mesh):
    in_specs = (
        P("orb", None, "aux"),
        P("orb", None, None, None),
        P("orb", None),
        P("aux", None, None),
        P("aux", None),
    )
    body = functools.partial(shards, mesh.shape["orb"], mesh.shape["aux"])
    return jax.shard_map(body, mesh=mesh, in_specs=in_specs, out_specs=P("orb", "aux", None), check_vma=False)
```

```python
import functools

import jax
import jax.numpy as jnp
from jax import lax
from jax.experimental import pallas as pl
from jax.experimental.pallas import tpu as pltpu
from jax.sharding import PartitionSpec as P

VMEM_WHOLE = 58 * 1024 * 1024
VMEM_MOST = 30 * 1024 * 1024
VMEM_LAST = 16 * 1024 * 1024
VMEM_PART = 44 * 1024 * 1024
SMALL = pl.CostEstimate(flops=0, bytes_accessed=4096, transcendentals=0)


def largest_divisor(total, most):
    return max(size for size in range(1, most + 1) if total % size == 0)


def pack_kernel(width, first, source, *chunks):
    half = source.shape[1] // 2
    for at, chunk in enumerate(chunks):
        columns = slice(first + at * width, first + (at + 1) * width)
        chunk[...] = jnp.concatenate([source[:, :half, columns], source[:, half:, columns]], axis=-1)


def pack_chunks(factors, width, begin, count):
    orbitals, domain, part = factors.shape
    first = begin * width
    lanes = min(part, 2 * width) if first + count * width <= 2 * width else part
    step = largest_divisor(orbitals, 12)
    packed = (step, domain // 2, 2 * width)
    return pl.pallas_call(
        functools.partial(pack_kernel, width, first),
        grid=(orbitals // step,),
        in_specs=[pl.BlockSpec((step, domain, lanes), lambda i: (i, 0, 0))],
        out_specs=[pl.BlockSpec(packed, lambda i: (i, 0, 0))] * count,
        out_shape=[jax.ShapeDtypeStruct((orbitals,) + packed[1:], factors.dtype)] * count,
        cost_estimate=SMALL,
        compiler_params=pltpu.CompilerParams(vmem_limit_bytes=VMEM_PART if begin else VMEM_WHOLE),
        name="pack_chunks",
    )(factors)


def halves_apart(one, two, half):
    lower = jnp.concatenate([one[:, :half], two[:, :half]], axis=1)
    upper = jnp.concatenate([one[:, half:], two[:, half:]], axis=1)
    return lower, upper


def product_kernel(pairs, split_rows, streams, slots, *refs):
    amplitudes, pieces = refs[: 2 * streams], refs[2 * streams : -3]
    out, table, arrived = refs[-3:]
    group, half_domain, lanes = pieces[0].shape
    here = pl.program_id(0)

    @pl.when(here == 0)
    def _():
        copies = [
            pltpu.make_async_copy(piece, table.at[pl.ds(at * group, group)], arrived.at[at])
            for at, piece in enumerate(pieces)
        ]
        for copy in copies:
            copy.start()
        for copy in copies:
            copy.wait()

    step, domain = amplitudes[0].shape[1], amplitudes[0].shape[3]
    each = pairs // streams
    half_count = pl.num_programs(0) * step
    first = lax.broadcasted_iota(jnp.int32, (domain, lanes), 1) < lanes // 2
    for q in range(step):
        sums = []
        for side in range(2):
            base = (side * half_count + here * step + q) * pairs
            lower, upper = [], []
            for k in range(0, pairs, 2):
                tiles = amplitudes[side * streams + k // each]
                low, high = halves_apart(tiles[0, q, k % each], tiles[0, q, k % each + 1], half_domain)
                lower.append(low)
                upper.append(high)
            left = jnp.concatenate([jnp.concatenate(lower, axis=1), jnp.concatenate(upper, axis=1)], axis=0)
            right = jnp.concatenate([table[slots[base + k]] for k in range(pairs)], axis=0)
            sums.append(jnp.dot(left, right, preferred_element_type=jnp.float32))
        placed = jnp.where(first, sums[0][:domain], sums[1][domain:])
        moved = jnp.where(first, sums[1][:domain], sums[0][domain:])
        both = (placed + pltpu.roll(moved, lanes // 2, 1)).astype(out.dtype)
        if split_rows:
            owners, rows = out.shape[0], domain // out.shape[0]
            out[:, q * rows : (q + 1) * rows, :] = both.reshape(owners, rows, lanes)
        else:
            out[q] = both


def chunk_products(slots, amplitudes, pieces, owners):
    orbitals, pairs, domain, _ = amplitudes.shape
    group, half_domain, lanes = pieces[0].shape
    total = group * len(pieces)
    half = orbitals // 2
    rows = domain // owners
    split_rows = rows % 16 == 0
    step = largest_divisor(half, 4)
    streams = 2 if pairs % 4 == 0 else 1
    tiles = (1, step, pairs // streams, domain, domain)
    if split_rows:
        out_shape, out_block, out_at = (owners, half * rows, lanes), (owners, step * rows, lanes), lambda i, s: (0, i, 0)
    else:
        out_shape, out_block, out_at = (half, domain, lanes), (step, domain, lanes), lambda i, s: (i, 0, 0)
    result = pl.pallas_call(
        functools.partial(product_kernel, pairs, split_rows, streams),
        grid_spec=pltpu.PrefetchScalarGridSpec(
            num_scalar_prefetch=1,
            grid=(half // step,),
            in_specs=[
                pl.BlockSpec(tiles, lambda i, s, side=side, part=part: (side, i, part, 0, 0))
                for side in range(2)
                for part in range(streams)
            ]
            + [pl.BlockSpec(memory_space=pl.ANY)] * len(pieces),
            out_specs=pl.BlockSpec(out_block, out_at),
            scratch_shapes=[
                pltpu.VMEM((total, half_domain, lanes), jnp.bfloat16),
                pltpu.SemaphoreType.DMA((len(pieces),)),
            ],
        ),
        out_shape=jax.ShapeDtypeStruct(out_shape, jnp.bfloat16),
        cost_estimate=SMALL,
        compiler_params=pltpu.CompilerParams(vmem_limit_bytes=VMEM_PART),
        name="chunk_products",
    )(slots, *[amplitudes.reshape(2, half, pairs, domain, domain)] * (2 * streams), *pieces)
    if split_rows:
        return result
    result = result.reshape(half, owners, rows, lanes).transpose(1, 0, 2, 3)
    return result.reshape(owners, half * rows, lanes)


def place_tiles(chunks, owners, tiles_each, positions, sources, dense):
    devices, _, span = sources[0].shape
    width = span // 2
    dense[...] = jnp.zeros_like(dense)
    for which, source in enumerate(sources):

        @pl.loop(0, devices)
        def _(device):
            for at in range(tiles_each):
                number = (which * devices + device) * tiles_each + at
                column = pl.multiple_of(positions[2 * number + 1] * span, span)
                for side in range(2):
                    block = 2 * positions[2 * number] + side
                    row = ((block % chunks) * owners + block // chunks) * width
                    begin = at * span + side * width
                    dense[pl.ds(pl.multiple_of(row, width), width), pl.ds(column, span)] = source[
                        device, begin : begin + width, :
                    ]


def unpack_rows(chunks, rows):
    owners, height, lanes = chunks[0].shape
    width = lanes // 2
    for at, chunk in enumerate(chunks):
        for owner in range(0, owners, 2):
            one, two = chunk[owner], chunk[owner + 1]
            columns = pl.ds((at * owners + owner) * width, lanes)
            rows[:height, columns] = jnp.concatenate([one[:, :width], two[:, :width]], axis=1)
            rows[height:, columns] = jnp.concatenate([one[:, width:], two[:, width:]], axis=1)


def first_kernel(count, source_count, tiles_each, positions, *refs):
    chunks, sources = refs[:count], refs[count : count + source_count]
    *outs, dense, rows = refs[count + source_count :]
    owners, height, _ = chunks[0].shape
    depth = rows.shape[1]

    @pl.when(pl.program_id(0) == 0)
    def _():
        place_tiles(dense.shape[0] // (depth // count), owners, tiles_each, positions, sources, dense)
        unpack_rows(chunks, rows)

    step = dense.shape[1] // pl.num_programs(0)
    columns = pl.ds(pl.multiple_of(pl.program_id(0) * step, step), step)
    if len(outs) > 1:
        outs[1][:, columns] = dense[depth:, columns]
    sums = jnp.dot(rows[...], dense[:depth, columns], preferred_element_type=jnp.float32)
    outs[0][:, columns] = sums.astype(outs[0].dtype)


def first_shares(chunks, positions, sources, tiles_each, size, dtype):
    owners, height, lanes = chunks[0].shape
    depth = len(chunks) * owners * lanes // 2
    step = largest_divisor(size, 256)
    whole = lambda j, s: (0, 0, 0)
    heights = [2 * height] + ([size - depth] if depth < size else [])
    kinds = [dtype, sources[0].dtype]
    return pl.pallas_call(
        functools.partial(first_kernel, len(chunks), len(sources), tiles_each),
        grid_spec=pltpu.PrefetchScalarGridSpec(
            num_scalar_prefetch=1,
            grid=(size // step,),
            in_specs=[pl.BlockSpec(array.shape, whole) for array in [*chunks, *sources]],
            out_specs=[pl.BlockSpec(memory_space=pltpu.VMEM)] * len(heights),
            scratch_shapes=[
                pltpu.VMEM((size, size), sources[0].dtype),
                pltpu.VMEM((2 * height, depth), jnp.bfloat16),
            ],
        ),
        out_shape=[pltpu.VMEM((tall, size), kind) for tall, kind in zip(heights, kinds)],
        cost_estimate=SMALL,
        compiler_params=pltpu.CompilerParams(vmem_limit_bytes=VMEM_MOST),
        name="first_shares",
    )(positions, *chunks, *sources)


def last_kernel(chunk, metric, before, out, rows):
    height = chunk.shape[1]

    @pl.when(pl.program_id(0) == 0)
    def _():
        unpack_rows([chunk], rows)

    step = out.shape[-1]
    columns = pl.ds(pl.multiple_of(pl.program_id(0) * step, step), step)
    sums = jnp.dot(rows[...], metric[:, columns], preferred_element_type=jnp.float32) + before[:, columns]
    out[0] = sums[:height].astype(out.dtype)
    out[1] = sums[height:].astype(out.dtype)


def last_share(chunk, metric, before):
    owners, height, lanes = chunk.shape
    depth, size = metric.shape
    step = largest_divisor(size, 256)
    return pl.pallas_call(
        last_kernel,
        grid=(size // step,),
        in_specs=[
            pl.BlockSpec(chunk.shape, lambda j: (0, 0, 0)),
            pl.BlockSpec(memory_space=pltpu.VMEM),
            pl.BlockSpec(memory_space=pltpu.VMEM),
        ],
        out_specs=pl.BlockSpec((2, height, step), lambda j: (0, 0, j)),
        out_shape=jax.ShapeDtypeStruct((2, height, size), jnp.bfloat16),
        scratch_shapes=[pltpu.VMEM((2 * height, depth), jnp.bfloat16)],
        cost_estimate=SMALL,
        compiler_params=pltpu.CompilerParams(vmem_limit_bytes=VMEM_LAST),
        name="last_share",
    )(chunk, metric, before)


def after(value, others):
    return lax.optimization_barrier((value, others))[0]


def shards(orb_count, aux_count, factors, amplitudes, partners, metric_tiles, tile_pos):
    group, domain, part = factors.shape
    span = metric_tiles.shape[1]
    width = span // 2
    chunk_count = part // width
    far_count = orb_count // 2
    me = lax.axis_index("orb")

    def to_far(array, shift):
        moves = [(g, (g + 2 * shift) % orb_count) for g in range(orb_count)]
        return lax.ppermute(array, "orb", moves)

    def to_mate(array):
        return lax.ppermute(array, "orb", [(g, g ^ 1) for g in range(orb_count)])

    owner, place = partners // group, partners % group
    far = (me // 2 - owner // 2) % far_count
    slots = ((far * 2 + (me % 2 + owner) % 2) * group + place).reshape(-1)

    half_tiles = metric_tiles.shape[0] // 2
    mine = (me % 2) * half_tiles
    tiles = lax.dynamic_slice_in_dim(metric_tiles, mine, half_tiles, axis=0).reshape(half_tiles * span, span)
    spots = lax.dynamic_slice_in_dim(tile_pos, mine, half_tiles, axis=0).reshape(-1).astype(tiles.dtype)
    spot_rows = -(-spots.size // (16 * span)) * 16
    spots = jnp.pad(spots, (0, spot_rows * span - spots.size)).reshape(spot_rows, span)
    load = jnp.concatenate([tiles, spots], axis=0)
    first = lax.all_gather(load[None], "aux", axis=0, tiled=True)
    sources = [first, to_mate(first)]

    packed = list(pack_chunks(factors, width, 0, 1))
    if chunk_count > 1:
        packed += pack_chunks(factors, width, 1, chunk_count - 1)

    before_products = {3: sources}
    products = []
    far_pieces, made = [], None
    for at in range(chunk_count):
        own = packed[at]
        if at:
            own = after(own, far_pieces)
        far_pieces = [to_far(own, shift) for shift in range(1, far_count)]
        if chunk_count > 1:
            far_pieces = after(far_pieces, made if at else packed[1:])
        pieces = []
        for piece in [packed[at]] + far_pieces:
            pieces += [piece, to_mate(piece)]
        places = after(slots, before_products[at]) if at in before_products else slots
        made = chunk_products(places, amplitudes, pieces, aux_count)
        products.append(lax.all_to_all(made, "aux", split_axis=0, concat_axis=0, tiled=True))

    positions = jnp.concatenate([source[:, half_tiles * span, : 2 * half_tiles] for source in sources])
    positions = positions.astype(jnp.int32).reshape(-1)
    size = part * aux_count
    if chunk_count > 1:
        ready = after(products[:-1], made)
        before, metric = first_shares(ready, positions, sources, half_tiles, size, jnp.float32)
        result = last_share(products[-1], metric, before)
    else:
        result = first_shares(products, positions, sources, half_tiles, size, jnp.bfloat16)[0]
        result = result.reshape(2, group // 2, domain // aux_count, size)
    return result.reshape(group, domain // aux_count, size)


def solution(mesh):
    in_specs = (
        P("orb", None, "aux"),
        P("orb", None, None, None),
        P("orb", None),
        P("aux", None, None),
        P("aux", None),
    )
    body = functools.partial(shards, mesh.shape["orb"], mesh.shape["aux"])
    return jax.shard_map(body, mesh=mesh, in_specs=in_specs, out_specs=P("orb", "aux", None), check_vma=False)
```

```python
import functools

import jax
import jax.numpy as jnp
from jax import lax
from jax.experimental import pallas as pl
from jax.experimental.pallas import tpu as pltpu
from jax.sharding import PartitionSpec as P

VMEM_WHOLE = 58 * 1024 * 1024
VMEM_MOST = 30 * 1024 * 1024
VMEM_PART = 44 * 1024 * 1024
SMALL = pl.CostEstimate(flops=0, bytes_accessed=4096, transcendentals=0)


def largest_divisor(total, most):
    return max(size for size in range(1, most + 1) if total % size == 0)


def pack_kernel(width, first, source, *chunks):
    half = source.shape[1] // 2
    for at, chunk in enumerate(chunks):
        columns = slice(first + at * width, first + (at + 1) * width)
        chunk[...] = jnp.concatenate([source[:, :half, columns], source[:, half:, columns]], axis=-1)


def pack_chunks(factors, width, begin, count):
    orbitals, domain, part = factors.shape
    first = begin * width
    lanes = min(part, 2 * width) if first + count * width <= 2 * width else part
    step = largest_divisor(orbitals, 12)
    packed = (step, domain // 2, 2 * width)
    return pl.pallas_call(
        functools.partial(pack_kernel, width, first),
        grid=(orbitals // step,),
        in_specs=[pl.BlockSpec((step, domain, lanes), lambda i: (i, 0, 0))],
        out_specs=[pl.BlockSpec(packed, lambda i: (i, 0, 0))] * count,
        out_shape=[jax.ShapeDtypeStruct((orbitals,) + packed[1:], factors.dtype)] * count,
        cost_estimate=SMALL,
        compiler_params=pltpu.CompilerParams(vmem_limit_bytes=VMEM_PART if begin else VMEM_WHOLE),
        name="pack_chunks",
    )(factors)


def halves_apart(one, two, half):
    lower = jnp.concatenate([one[:, :half], two[:, :half]], axis=1)
    upper = jnp.concatenate([one[:, half:], two[:, half:]], axis=1)
    return lower, upper


def product_kernel(pairs, split_rows, streams, slots, *refs):
    amplitudes, pieces = refs[: 2 * streams], refs[2 * streams : -3]
    out, table, arrived = refs[-3:]
    group, half_domain, lanes = pieces[0].shape
    here = pl.program_id(0)

    @pl.when(here == 0)
    def _():
        copies = [
            pltpu.make_async_copy(piece, table.at[pl.ds(at * group, group)], arrived.at[at])
            for at, piece in enumerate(pieces)
        ]
        for copy in copies:
            copy.start()
        for copy in copies:
            copy.wait()

    step, domain = amplitudes[0].shape[1], amplitudes[0].shape[3]
    each = pairs // streams
    half_count = pl.num_programs(0) * step
    first = lax.broadcasted_iota(jnp.int32, (domain, lanes), 1) < lanes // 2
    for q in range(step):
        sums = []
        for side in range(2):
            base = (side * half_count + here * step + q) * pairs
            lower, upper = [], []
            for k in range(0, pairs, 2):
                tiles = amplitudes[side * streams + k // each]
                low, high = halves_apart(tiles[0, q, k % each], tiles[0, q, k % each + 1], half_domain)
                lower.append(low)
                upper.append(high)
            left = jnp.concatenate([jnp.concatenate(lower, axis=1), jnp.concatenate(upper, axis=1)], axis=0)
            right = jnp.concatenate([table[slots[base + k]] for k in range(pairs)], axis=0)
            sums.append(jnp.dot(left, right, preferred_element_type=jnp.float32))
        placed = jnp.where(first, sums[0][:domain], sums[1][domain:])
        moved = jnp.where(first, sums[1][:domain], sums[0][domain:])
        both = (placed + pltpu.roll(moved, lanes // 2, 1)).astype(out.dtype)
        if split_rows:
            owners, rows = out.shape[0], domain // out.shape[0]
            out[:, q * rows : (q + 1) * rows, :] = both.reshape(owners, rows, lanes)
        else:
            out[q] = both


def chunk_products(slots, amplitudes, pieces, owners):
    orbitals, pairs, domain, _ = amplitudes.shape
    group, half_domain, lanes = pieces[0].shape
    total = group * len(pieces)
    half = orbitals // 2
    rows = domain // owners
    split_rows = rows % 16 == 0
    step = largest_divisor(half, 4)
    streams = 2 if pairs % 4 == 0 else 1
    tiles = (1, step, pairs // streams, domain, domain)
    if split_rows:
        out_shape, out_block, out_at = (owners, half * rows, lanes), (owners, step * rows, lanes), lambda i, s: (0, i, 0)
    else:
        out_shape, out_block, out_at = (half, domain, lanes), (step, domain, lanes), lambda i, s: (i, 0, 0)
    result = pl.pallas_call(
        functools.partial(product_kernel, pairs, split_rows, streams),
        grid_spec=pltpu.PrefetchScalarGridSpec(
            num_scalar_prefetch=1,
            grid=(half // step,),
            in_specs=[
                pl.BlockSpec(tiles, lambda i, s, side=side, part=part: (side, i, part, 0, 0))
                for side in range(2)
                for part in range(streams)
            ]
            + [pl.BlockSpec(memory_space=pl.ANY)] * len(pieces),
            out_specs=pl.BlockSpec(out_block, out_at),
            scratch_shapes=[
                pltpu.VMEM((total, half_domain, lanes), jnp.bfloat16),
                pltpu.SemaphoreType.DMA((len(pieces),)),
            ],
        ),
        out_shape=jax.ShapeDtypeStruct(out_shape, jnp.bfloat16),
        cost_estimate=SMALL,
        compiler_params=pltpu.CompilerParams(vmem_limit_bytes=VMEM_PART),
        name="chunk_products",
    )(slots, *[amplitudes.reshape(2, half, pairs, domain, domain)] * (2 * streams), *pieces)
    if split_rows:
        return result
    result = result.reshape(half, owners, rows, lanes).transpose(1, 0, 2, 3)
    return result.reshape(owners, half * rows, lanes)


def place_tiles(chunks, owners, tiles_each, positions, sources, dense):
    devices, _, span = sources[0].shape
    width = span // 2
    dense[...] = jnp.zeros_like(dense)
    for which, source in enumerate(sources):

        @pl.loop(0, devices)
        def _(device):
            for at in range(tiles_each):
                number = (which * devices + device) * tiles_each + at
                column = pl.multiple_of(positions[2 * number + 1] * span, span)
                for side in range(2):
                    block = 2 * positions[2 * number] + side
                    row = ((block % chunks) * owners + block // chunks) * width
                    begin = at * span + side * width
                    dense[pl.ds(pl.multiple_of(row, width), width), pl.ds(column, span)] = source[
                        device, begin : begin + width, :
                    ]


def unpack_rows(chunks, rows):
    owners, height, lanes = chunks[0].shape
    width = lanes // 2
    for at, chunk in enumerate(chunks):
        for owner in range(0, owners, 2):
            one, two = chunk[owner], chunk[owner + 1]
            columns = pl.ds((at * owners + owner) * width, lanes)
            rows[:height, columns] = jnp.concatenate([one[:, :width], two[:, :width]], axis=1)
            rows[height:, columns] = jnp.concatenate([one[:, width:], two[:, width:]], axis=1)


def first_kernel(count, source_count, tiles_each, positions, *refs):
    chunks, sources = refs[:count], refs[count : count + source_count]
    *outs, dense, rows = refs[count + source_count :]
    owners, height, _ = chunks[0].shape
    depth = rows.shape[1]

    @pl.when(pl.program_id(0) == 0)
    def _():
        place_tiles(dense.shape[0] // (depth // count), owners, tiles_each, positions, sources, dense)
        unpack_rows(chunks, rows)

    step = dense.shape[1] // pl.num_programs(0)
    columns = pl.ds(pl.multiple_of(pl.program_id(0) * step, step), step)
    if len(outs) > 1:
        outs[1][...] = dense[depth:, columns]
    sums = jnp.dot(rows[...], dense[:depth, columns], preferred_element_type=jnp.float32)
    outs[0][...] = sums.astype(outs[0].dtype)


def first_shares(chunks, positions, sources, tiles_each, size, dtype):
    owners, height, lanes = chunks[0].shape
    depth = len(chunks) * owners * lanes // 2
    step = largest_divisor(size, 256)
    whole = lambda j, s: (0, 0, 0)
    heights = [2 * height] + ([size - depth] if depth < size else [])
    kinds = [dtype, sources[0].dtype]
    return pl.pallas_call(
        functools.partial(first_kernel, len(chunks), len(sources), tiles_each),
        grid_spec=pltpu.PrefetchScalarGridSpec(
            num_scalar_prefetch=1,
            grid=(size // step,),
            in_specs=[pl.BlockSpec(array.shape, whole) for array in [*chunks, *sources]],
            out_specs=[pl.BlockSpec((tall, step), lambda j, s: (0, j)) for tall in heights],
            scratch_shapes=[
                pltpu.VMEM((size, size), sources[0].dtype),
                pltpu.VMEM((2 * height, depth), jnp.bfloat16),
            ],
        ),
        out_shape=[jax.ShapeDtypeStruct((tall, size), kind) for tall, kind in zip(heights, kinds)],
        cost_estimate=SMALL,
        compiler_params=pltpu.CompilerParams(vmem_limit_bytes=VMEM_MOST),
        name="first_shares",
    )(positions, *chunks, *sources)


def last_kernel(chunk, metric, before, out, rows):
    @pl.when(pl.program_id(0) == 0)
    def _():
        unpack_rows([chunk], rows)

    step = out.shape[0]
    part = rows[pl.ds(pl.multiple_of(pl.program_id(0) * step, step), step), :]
    sums = jnp.dot(part, metric[...], preferred_element_type=jnp.float32) + before[...]
    out[...] = sums.astype(out.dtype)


def last_share(chunk, metric, before):
    height, size = before.shape
    depth = metric.shape[0]
    step = largest_divisor(height // 16, 12) * 16
    rows = pl.BlockSpec((step, size), lambda j: (j, 0))
    return pl.pallas_call(
        last_kernel,
        grid=(height // step,),
        in_specs=[
            pl.BlockSpec(chunk.shape, lambda j: (0, 0, 0)),
            pl.BlockSpec((depth, size), lambda j: (0, 0)),
            rows,
        ],
        out_specs=rows,
        out_shape=jax.ShapeDtypeStruct((height, size), jnp.bfloat16),
        scratch_shapes=[pltpu.VMEM((height, depth), jnp.bfloat16)],
        cost_estimate=SMALL,
        compiler_params=pltpu.CompilerParams(vmem_limit_bytes=VMEM_WHOLE),
        name="last_share",
    )(chunk, metric, before)


def after(value, others):
    return lax.optimization_barrier((value, others))[0]


def shards(orb_count, aux_count, factors, amplitudes, partners, metric_tiles, tile_pos):
    group, domain, part = factors.shape
    span = metric_tiles.shape[1]
    width = span // 2
    chunk_count = part // width
    far_count = orb_count // 2
    me = lax.axis_index("orb")

    def to_far(array, shift):
        moves = [(g, (g + 2 * shift) % orb_count) for g in range(orb_count)]
        return lax.ppermute(array, "orb", moves)

    def to_mate(array):
        return lax.ppermute(array, "orb", [(g, g ^ 1) for g in range(orb_count)])

    owner, place = partners // group, partners % group
    far = (me // 2 - owner // 2) % far_count
    slots = ((far * 2 + (me % 2 + owner) % 2) * group + place).reshape(-1)

    half_tiles = metric_tiles.shape[0] // 2
    mine = (me % 2) * half_tiles
    tiles = lax.dynamic_slice_in_dim(metric_tiles, mine, half_tiles, axis=0).reshape(half_tiles * span, span)
    spots = lax.dynamic_slice_in_dim(tile_pos, mine, half_tiles, axis=0).reshape(-1).astype(tiles.dtype)
    spot_rows = -(-spots.size // (16 * span)) * 16
    spots = jnp.pad(spots, (0, spot_rows * span - spots.size)).reshape(spot_rows, span)
    load = jnp.concatenate([tiles, spots], axis=0)
    first = lax.all_gather(load[None], "aux", axis=0, tiled=True)
    sources = [first, to_mate(first)]

    packed = list(pack_chunks(factors, width, 0, 1))
    if chunk_count > 1:
        packed += pack_chunks(factors, width, 1, chunk_count - 1)

    before_products = {3: sources}
    products = []
    far_pieces, made = [], None
    for at in range(chunk_count):
        own = packed[at]
        if at:
            own = after(own, far_pieces)
        far_pieces = [to_far(own, shift) for shift in range(1, far_count)]
        if chunk_count > 1:
            far_pieces = after(far_pieces, made if at else packed[1:])
        pieces = []
        for piece in [packed[at]] + far_pieces:
            pieces += [piece, to_mate(piece)]
        places = after(slots, before_products[at]) if at in before_products else slots
        made = chunk_products(places, amplitudes, pieces, aux_count)
        products.append(lax.all_to_all(made, "aux", split_axis=0, concat_axis=0, tiled=True))

    positions = jnp.concatenate([source[:, half_tiles * span, : 2 * half_tiles] for source in sources])
    positions = positions.astype(jnp.int32).reshape(-1)
    size = part * aux_count
    if chunk_count > 1:
        ready = after(products[:-1], made)
        before, metric = first_shares(ready, positions, sources, half_tiles, size, jnp.float32)
        result = last_share(products[-1], metric, before)
    else:
        result = first_shares(products, positions, sources, half_tiles, size, jnp.bfloat16)[0]
    return result.reshape(group, domain // aux_count, size)


def solution(mesh):
    in_specs = (
        P("orb", None, "aux"),
        P("orb", None, None, None),
        P("orb", None),
        P("aux", None, None),
        P("aux", None),
    )
    body = functools.partial(shards, mesh.shape["orb"], mesh.shape["aux"])
    return jax.shard_map(body, mesh=mesh, in_specs=in_specs, out_specs=P("orb", "aux", None), check_vma=False)
```
